128 devices in a mesh: tm: 16 (over x, z_lo, core), height: 4 (over y), mp: 2 (over z_hi).
Axes of the slice: x: 4, y: 4, z: 4 (z_hi: 2, z_lo: 2; z = z_hi * 2 + z_lo), core: 2. Of those that a mesh axis runs over, the one named last changes fastest.
Arguments:
- tokens: bfloat16 [32, 8, 48, 3072], P('tm', 'height'), may hold values from -60 to 60
- tangent: bfloat16 [32, 8, 48, 3072], P('tm', 'height'), may hold values from -6 to 6
- qkv_weight: bfloat16 [3072, 3, 1536], P('tm', None, 'mp'), may hold values from -0.109375 to 0.109375
- out_weight: bfloat16 [1536, 3072], P('mp', 'tm'), may hold values from -0.15625 to 0.15625
- reach: int32 [2, 12], P(None, 'mp'), may hold values from 0 to 1
Outputs:
- result: bfloat16 [32, 8, 48, 3072], P('tm', 'height', None, 'mp')
- result_tangent: bfloat16 [32, 8, 48, 3072], P('tm', 'height', None, 'mp')
The draws below stay inside these ranges and needn't reach their ends.
All inputs are finite; a program needn't handle non-finite values.
Results may differ from the reference program's by a relative error of at most 0.024.
The reference program's roundings to bfloat16 on the way count: a program that leaves them out, or rounds other values in their place, can miss the bound.
Values may be sent and summed in bfloat16 or wider, within the bound.
A program may use at most 128 MiB of HBM per device.

```python
import jax
import jax.numpy as jnp
from jax import lax

D = 3072
HEADS = 12
DH = 128
SIDE = 2
COLS = 48
FRAMES = 32
ROWS = 8
N_TM = 16
N_HEIGHT = 4


def draw_tokens(key, part):
    key = jax.random.fold_in(key, 11)
    normal_key = jax.random.fold_in(key, 0)
    base = jax.random.truncated_normal(normal_key, -6.0, 6.0, (FRAMES, ROWS, COLS, D), jnp.float32)
    return base.astype(jnp.bfloat16)


def set_ends(entries, stream_key, low, high):
    index_at = [jax.random.randint(jax.random.fold_in(stream_key, axis), (), 0, length) for axis, length in enumerate(entries.shape)]
    longest = entries.shape.index(max(entries.shape))
    next_to = index_at[:longest] + [(index_at[longest] + 1) % entries.shape[longest]] + index_at[longest + 1:]
    return entries.at[tuple(index_at)].set(low).at[tuple(next_to)].set(high)


def block_scale(rng, shape, cuts, smallest, largest):
    def one(axis_at, shards_of):
        steps = jax.random.uniform(jax.random.fold_in(jax.random.fold_in(rng, 6), axis_at), (shards_of,), jnp.float32, smallest / len(cuts), largest / len(cuts))
        return jnp.repeat(jnp.exp(steps), shape[axis_at] // shards_of).reshape((-1,) + (1,) * (len(shape) - axis_at - 1))

    gain = one(*cuts[0])
    for cut in cuts[1:]:
        gain = gain * one(*cut)
    return gain


def centred(rng, dims, width, most, cuts=(), held_as=jnp.bfloat16):
    level = block_scale(rng, dims, cuts, -0.22, 0.18) if cuts else 1.0
    array = jax.random.normal(rng, dims, jnp.float32) * width * level
    return jnp.minimum(jnp.maximum(array, -most), most).astype(held_as)


def setup_inputs(seed: int = 0) -> dict:
    key_of = jax.random.split(jax.random.key(seed), 6)
    tokens = draw_tokens(jax.random.fold_in(key_of[5], 71), 0)
    tangent = centred(key_of[1], (FRAMES, ROWS, COLS, D), 1.0, 6.0, ((0, 16), (1, 4)))
    qkv_weight = centred(key_of[2], (D, 3, HEADS * DH), D ** -0.5, 0.109375, ((0, 16), (2, 2)))
    out_weight = centred(key_of[3], (HEADS * DH, D), (HEADS * DH) ** -0.5, 0.15625, ((0, 2), (1, 16)))
    reach = set_ends(jax.random.randint(key_of[4], (2, HEADS), 0, 2), jax.random.fold_in(key_of[4], 1), 0, 1).astype(jnp.int32)
    return {"tokens": tokens, "tangent": tangent, "qkv_weight": qkv_weight, "out_weight": out_weight, "reach": reach}


def attend(query, query_move, key, key_move, value, value_move, allow):
    factor = 1.0 / (query.shape[-1] ** 0.5)
    scores = jnp.dot(query, key.T, preferred_element_type=jnp.float32) * factor
    slope = (jnp.dot(query_move, key.T, preferred_element_type=jnp.float32) + jnp.dot(query, key_move.T, preferred_element_type=jnp.float32)) * factor
    scores = jnp.where(allow[None, :], scores, jnp.float32(-1e30))
    top = jnp.max(scores, axis=-1, keepdims=True)
    weights = jnp.where(allow[None, :], jnp.exp(scores - top), jnp.float32(0.0))
    probs = weights / jnp.sum(weights, axis=-1, keepdims=True)
    probs_low = probs.astype(jnp.bfloat16)
    output = jnp.dot(probs_low, value, preferred_element_type=jnp.float32)
    moved = probs * slope
    shift = jnp.sum(moved, axis=-1, keepdims=True)
    output_move = jnp.dot(probs_low, value_move, preferred_element_type=jnp.float32) + jnp.dot(moved.astype(jnp.bfloat16), value, preferred_element_type=jnp.float32) - output * shift
    return output.astype(jnp.bfloat16), output_move.astype(jnp.bfloat16)


def reference(tokens, tangent, qkv_weight, out_weight, reach):
    cells = FRAMES * ROWS * COLS
    tile_rows = SIDE * SIDE * COLS
    stacked = jnp.concatenate([tokens.reshape(cells, D), tangent.reshape(cells, D)], 0)
    projected = jnp.dot(stacked, qkv_weight.reshape(D, 3 * HEADS * DH), preferred_element_type=jnp.float32).astype(jnp.bfloat16)
    projected = projected.reshape(2, FRAMES, ROWS, COLS, 3, HEADS, DH)
    padded = jnp.pad(projected, ((0, 0), (SIDE, SIDE), (SIDE, SIDE), (0, 0), (0, 0), (0, 0), (0, 0)))
    block = (jnp.arange(3 * SIDE) // SIDE - 1).astype(jnp.int32)

    def tile(index):
        frame_tile = (index // N_HEIGHT).astype(jnp.int32)
        row_tile = (index % N_HEIGHT).astype(jnp.int32)
        zero = jnp.int32(0)
        window = lax.dynamic_slice(padded, (zero, frame_tile * SIDE, row_tile * SIDE, zero, zero, zero, zero), (2, 3 * SIDE, 3 * SIDE, COLS, 3, HEADS, DH))
        center = window[:, SIDE:2 * SIDE, SIDE:2 * SIDE, :, 0].reshape(2, tile_rows, HEADS, DH)
        keys = window[:, :, :, :, 1:].reshape(2, 9 * tile_rows, 2, HEADS, DH)
        frame_ok = (frame_tile + block >= 0) & (frame_tile + block < N_TM)
        row_ok = (row_tile + block >= 0) & (row_tile + block < N_HEIGHT)
        allow_frames = (jnp.abs(block)[None, :] <= reach[0][:, None]) & frame_ok[None, :]
        allow_rows = (jnp.abs(block)[None, :] <= reach[1][:, None]) & row_ok[None, :]
        allow = allow_frames[:, :, None, None] & allow_rows[:, None, :, None]
        allow = jnp.broadcast_to(allow, (HEADS, 3 * SIDE, 3 * SIDE, COLS)).reshape(HEADS, 9 * tile_rows)
        query = jnp.transpose(center[0], (1, 0, 2))
        query_move = jnp.transpose(center[1], (1, 0, 2))
        key = jnp.transpose(keys[0, :, 0], (1, 0, 2))
        value = jnp.transpose(keys[0, :, 1], (1, 0, 2))
        key_move = jnp.transpose(keys[1, :, 0], (1, 0, 2))
        value_move = jnp.transpose(keys[1, :, 1], (1, 0, 2))
        return lax.map(lambda items: attend(*items), (query, query_move, key, key_move, value, value_move, allow))

    output, output_move = lax.map(tile, jnp.arange(N_TM * N_HEIGHT, dtype=jnp.int32))

    def arrange(heads_out):
        grid = heads_out.reshape(N_TM, N_HEIGHT, HEADS, SIDE, SIDE, COLS, DH)
        grid = jnp.transpose(grid, (0, 3, 1, 4, 5, 2, 6))
        return grid.reshape(cells, HEADS * DH)

    hidden = jnp.concatenate([arrange(output), arrange(output_move)], 0)
    mixed = jnp.dot(hidden, out_weight, preferred_element_type=jnp.float32).astype(jnp.bfloat16)
    result = mixed[:cells].reshape(FRAMES, ROWS, COLS, D)
    result_tangent = mixed[cells:].reshape(FRAMES, ROWS, COLS, D)
    return result, result_tangent
```

```python
import jax
import jax.numpy as jnp
from jax import lax
from jax.experimental import pallas as pl
from jax.experimental.pallas import tpu as pltpu
from jax.sharding import PartitionSpec as P

MESH = pl.DeviceIdType.MESH
T = 192
D = 3072
QT = 48
BF = jnp.bfloat16
F32 = jnp.float32


def kernel(reach, tok, tan, wq, wot, out, tk, w, kv, qb, hs, hid, wz, wo, lsem, ss, rs, ysem, xsem, csem, hsem):
    tm = lax.axis_index("tm")
    y = lax.axis_index("height")
    mp = lax.axis_index("mp")
    x = lax.div(tm, 4)
    zl = lax.rem(lax.div(tm, 2), 2)
    c = lax.rem(tm, 2)
    z = 2 * mp + zl
    oz = 1 - zl
    df = 1 - 2 * c

    def wrap(i):
        return lax.rem(i + 4, 4)

    def dev(xx, yy, zz, cc):
        return (wrap(xx) * 4 + lax.rem(zz, 2) * 2 + cc, wrap(yy), lax.div(zz, 2))

    sib = dev(x, y, z, 1 - c)
    zin = dev(x, y, 2 * mp + oz, c)
    zout = dev(x, y, 2 * (1 - mp) + oz, c)
    zfar = dev(x, y, 2 * (1 - mp) + zl, c)
    xf, xb = dev(x + df, y, z, c), dev(x - df, y, z, c)
    xfar = dev(x + 2, y, z, c)
    xp = dev(x - df, y, z, 1 - c)
    yf, yb = dev(x, y + df, z, c), dev(x, y - df, z, c)
    yup, ydn = dev(x, y + 1, z, c), dev(x, y - 1, z, c)

    peers = (sib, zin, zout, zfar, xf, xb, xfar, xp, yf, yb)
    barrier = pltpu.get_barrier_semaphore()
    for p in peers:
        pl.semaphore_signal(barrier, inc=1, device_id=p, device_id_type=MESH)

    mine = [
        pltpu.make_async_copy(wq.at[zl], w.at[x, zl, c], lsem.at[0]),
        pltpu.make_async_copy(tok, tk.at[0, 0], lsem.at[1]),
        pltpu.make_async_copy(tan, tk.at[0, 1], lsem.at[2]),
        pltpu.make_async_copy(
            wot.at[pl.ds(pl.multiple_of(QT * y, QT), QT)], wz.at[zl, :, pl.ds(pl.multiple_of(mp * 768, 768), 768)], lsem.at[3]
        ),
    ]
    for m in mine:
        m.start()
    pl.semaphore_wait(barrier, len(peers))

    started, from_sib = [], []

    def put(src, dst, where, k):
        cp = pltpu.make_async_remote_copy(
            src_ref=src, dst_ref=dst, send_sem=ss.at[k], recv_sem=rs.at[k], device_id=where, device_id_type=MESH
        )
        cp.start()
        started.append(cp)
        if where is sib:
            from_sib.append(cp)
        return cp

    def rows(yy):
        return pl.ds(pl.multiple_of(QT * wrap(yy), QT), QT)

    yq = rows(y)
    z_w = put(wq.at[oz, yq], w.at[x, zl, c, yq], zin, 0)
    wzl = wz.at[zl, :, pl.ds(pl.multiple_of(mp * 768, 768), 768)]
    z_o = [put(wot.at[yq], wzl, d, 1 + i) for i, d in enumerate((zin, zout, zfar))]
    t0 = put(tok, tk.at[1, 0], zin, 4)
    t1 = put(tan, tk.at[1, 1], zout, 5)
    mine[0].wait()
    z_w.wait_recv()
    q_at = w.at[x, oz, c, yq]
    q_f, q_b = put(q_at, q_at, xf, 6), put(q_at, q_at, xb, 7)
    o_at = w.at[x, zl, c]
    o_f, o_b = put(o_at, o_at, xf, 8), put(o_at, o_at, xb, 9)
    put(o_at, o_at, sib, 10)
    q_f.wait_recv()
    q_at = w.at[wrap(x - df), oz, c, yq]
    q_o = put(q_at, q_at, xf, 11)
    q_b.wait_recv()
    q_o.wait_recv()
    q_at = w.at[:, oz, c, yq]
    y_f, y_b = put(q_at, q_at, yf, 12), put(q_at, q_at, yb, 13)
    put(q_at, q_at, sib, 14)
    o_f.wait_recv()
    o_at = w.at[wrap(x - df), zl, c]
    o_o = put(o_at, o_at, xf, 15)
    put(o_at, o_at, sib, 16)
    y_f.wait_recv()
    q_at = w.at[:, oz, c, rows(y - df)]
    y_o = put(q_at, q_at, yf, 17)
    put(q_at, q_at, sib, 18)
    o_b.wait_recv()
    o_at = w.at[wrap(x + df), zl, c]
    put(o_at, o_at, sib, 19)
    y_b.wait_recv()
    q_at = w.at[:, oz, c, rows(y + df)]
    put(q_at, q_at, sib, 20)
    mine[3].wait()
    for cp in z_o:
        cp.wait_recv()
    holder = lax.div(x, 2) == mp
    mine[1].wait()
    mine[2].wait()
    o_o.wait_recv()
    o_at = w.at[wrap(x + 2), zl, c]
    put(o_at, o_at, sib, 21)
    y_o.wait_recv()
    q_at = w.at[:, oz, c, rows(y + 2)]
    put(q_at, q_at, sib, 22)

    def wo_at(xx, yy):
        return wo.at[lax.rem(xx, 2), :, c, yy]

    def wo_x(d, k):
        return pltpu.make_async_remote_copy(
            src_ref=wz, dst_ref=wo_at(x, y), send_sem=ss.at[k], recv_sem=rs.at[k], device_id=d, device_id_type=MESH
        )

    wo_own = pltpu.make_async_copy(wz, wo_at(x, y), lsem.at[4])
    wo_sends = [wo_x(d, 23 + i) for i, d in enumerate((xf, xb, xfar))]

    @pl.when(holder)
    def _():
        wo_own.start()
        for cp in wo_sends:
            cp.start()

    for cp in from_sib:
        cp.wait_recv()

    def project(i, tau):
        b = 3 * (1 + 2 * tau) + 1

        def lanes(lo, n):
            lhs = tk[i].reshape(2 * T, D)
            return jnp.dot(lhs, w[:, :, :, :, lo : lo + n].reshape(D, n), preferred_element_type=F32).astype(BF)

        for half in range(3):
            r = lanes(384 + 256 * half, 256)
            for part in range(2):
                j = 2 * half + part
                at = (j % 3) * 512 + (j // 3) * 256
                kv[b, :, at : at + 128] = r[:T, part * 128 : part * 128 + 128]
                kv[b, :, at + 128 : at + 256] = r[T:, part * 128 : part * 128 + 128]
        return lanes

    def project_q(i, tau):
        lhs = tk[i].reshape(2 * T, D)
        r = jnp.dot(lhs, w[:, :, :, :, 0:384].reshape(D, 384), preferred_element_type=F32).astype(BF)
        for h in range(3):
            q, qm = r[:T, h * 128 : h * 128 + 128], r[T:, h * 128 : h * 128 + 128]
            qb[tau, h, :T, :128] = q
            qb[tau, h, :T, 128:] = jnp.zeros_like(q)
            qb[tau, h, T:, :128] = qm
            qb[tau, h, T:, 128:] = q

    def head(b, h):
        return kv.at[b, :, pl.ds(pl.multiple_of(h * 512, 512), 512)]

    def far(sems, idx, src, dst, where):
        return pltpu.make_async_remote_copy(
            src_ref=src,
            dst_ref=dst,
            send_sem=sems.at[(0,) + idx],
            recv_sem=sems.at[(1,) + idx],
            device_id=where,
            device_id_type=MESH,
        )

    def y_copy(tau, h, up):
        s = 3 * (1 + 2 * tau)
        return far(ysem, (tau, h, up), head(s + 1, h), head(s + 2 - 2 * up, h), yup if up else ydn)

    def sib_copy(tau, h, dh):
        s = 1 + 2 * tau
        return far(csem, (tau, h, dh), head(3 * s + dh, h), head(3 * (s - df) + dh, h), sib)

    def x_copy(h, dh):
        return far(xsem, (h, dh), head(3 * (1 + 2 * c) + dh, h), head(12 - 12 * c + dh, h), xp)

    def halo(tau):
        for h in range(3):
            y_copy(tau, h, 1).start()
            y_copy(tau, h, 0).start()
        for h in range(3):
            sib_copy(tau, h, 1).start()

    project(0, zl)
    halo(zl)
    project_q(0, zl)
    t0.wait_recv()
    t1.wait_recv()
    project(1, oz)
    halo(oz)
    for h in range(3):
        x_copy(h, 1).start()
    project_q(1, oz)

    for xr in range(2):
        d = lax.rem(2 * mp + xr - x + 4, 4)

        @pl.when(d == 0)
        def _():
            wo_own.wait()

        for i, step in enumerate((4 - df, 4 + df, jnp.int32(2))):

            @pl.when(d == lax.rem(step, 4))
            def _(i=i):
                wo_sends[i].wait_recv()

    quarter = wo.at[:, :, c, y]
    wy_f, wy_b = put(quarter, quarter, yf, 26), put(quarter, quarter, yb, 27)
    put(quarter, quarter, sib, 28)

    def attend(tau, h):
        k = kv[pl.ds(6 * tau, 9), :, pl.ds(pl.multiple_of(h * 512, 256), 256)].reshape(9 * T, 256)
        v = kv[pl.ds(6 * tau, 9), :, pl.ds(pl.multiple_of(h * 512 + 256, 256), 256)].reshape(9 * T, 256)
        both = lax.dot_general(qb[tau, h], k, (((1,), (1,)), ((), ())), preferred_element_type=F32)
        tile = 4 * x + 2 * tau + c
        hid_h = 3 * zl + h
        low = jnp.float32(-1e30)
        zero = jnp.float32(0.0)
        rf, rr = reach[0, hid_h], reach[1, hid_h]
        left = jnp.where((rf >= 1) & (tile > 0), zero, low)
        right = jnp.where((rf >= 1) & (tile < 15), zero, low)
        above = jnp.where((rr >= 1) & (y > 0), zero, low)
        below = jnp.where((rr >= 1) & (y < 3), zero, low)
        col = lax.broadcasted_iota(jnp.int32, (1, 9 * T), 1)
        bias = jnp.where(col < 3 * T, left, jnp.where(col >= 6 * T, right, zero))
        row = col - jnp.where(col < 3 * T, 0, jnp.where(col >= 6 * T, 6 * T, 3 * T))
        bias = bias + jnp.where(row < T, above, jnp.where(row >= 2 * T, below, zero))
        factor = 1.0 / 128**0.5
        s = both[:T] * factor + bias
        e = jnp.exp(s - jnp.max(s, axis=-1, keepdims=True))
        p = e * (1.0 / jnp.sum(e, axis=-1, keepdims=True))
        m = p * (both[T:] * factor)
        shift = jnp.sum(m, axis=-1, keepdims=True)
        lhs = jnp.concatenate([p.astype(BF), m.astype(BF)], 0)
        r = jnp.dot(lhs, v, preferred_element_type=F32)
        o = r[:T, :128]
        om = r[:T, 128:] + r[T:, :128] - o * shift
        at = pl.ds(pl.multiple_of(h * 128, 128), 128)
        hs[tau, :T, at] = o.astype(BF)
        hs[tau, T:, at] = om.astype(BF)

    def hid_copies(tau, h):
        at = pl.ds(pl.multiple_of(h * 128, 128), 128)
        src = hs.at[tau, :, at]
        dst = hid.at[:, pl.ds(pl.multiple_of(z * 384 + h * 128, 128), 128)]
        own = pltpu.make_async_copy(src, dst, lsem.at[5 + h])
        return own, [far(hsem, (i, h), src, dst, d) for i, d in enumerate((zin, zout, zfar))]

    def send_hidden(tau, h):
        own, (a, b, f) = hid_copies(tau, h)

        @pl.when(tau == zl)
        def _():
            own.start()
            f.start()

        @pl.when(tau != zl)
        def _():
            a.start()
            b.start()

    def first(h, carry):
        for up in range(2):
            y_copy(c, h, up).wait_recv()
        for dh in (0, 2):
            x_copy(h, dh).start()
            sib_copy(c, h, dh).start()
        for up in range(2):
            y_copy(1 - c, h, up).wait_recv()
        for dh in (0, 2):
            sib_copy(1 - c, h, dh).start()
        for tau in range(2):
            for dh in range(3):
                sib_copy(tau, h, dh).wait_recv()
        attend(1 - c, h)
        send_hidden(1 - c, h)
        return carry

    lax.fori_loop(0, 3, first, 0)

    wy_f.wait_recv()
    quarter = wo.at[:, :, c, wrap(y - df)]
    wy_o = put(quarter, quarter, yf, 29)
    put(quarter, quarter, sib, 30)

    def second(h, carry):
        for dh in range(3):
            x_copy(h, dh).wait_recv()
        attend(c, h)
        send_hidden(c, h)
        return carry

    lax.fori_loop(0, 3, second, 0)

    wy_b.wait_recv()
    quarter = wo.at[:, :, c, wrap(y + df)]
    put(quarter, quarter, sib, 31)
    wy_o.wait_recv()
    quarter = wo.at[:, :, c, wrap(y + 2)]
    put(quarter, quarter, sib, 32)
    for cp in from_sib[8:]:
        cp.wait_recv()

    for h in range(3):
        own, remote = hid_copies(zl, h)
        own.wait()
        for cp in remote:
            cp.wait_recv()

    for a in range(2):
        r = lax.dot_general(
            hid[...], wo[a].reshape(768, 1536), (((1,), (1,)), ((), ())), preferred_element_type=F32
        )
        out[:, a * 768 : a * 768 + 768] = r.astype(BF)

    for cp in started:
        cp.wait_send()

    @pl.when(holder)
    def _():
        for cp in wo_sends:
            cp.wait_send()

    def drain(h, carry):
        for tau in range(2):
            for up in range(2):
                y_copy(tau, h, up).wait_send()
            for dh in range(3):
                sib_copy(tau, h, dh).wait_send()
        for dh in range(3):
            x_copy(h, dh).wait_send()
        own, remote = hid_copies(zl, h)
        for cp in remote:
            cp.wait_send()
        return carry

    lax.fori_loop(0, 3, drain, 0)


def per_device(tokens, tangent, qkv_weight, out_weight, reach):
    any_spec = pl.BlockSpec(memory_space=pl.ANY)
    wq = jnp.transpose(qkv_weight.reshape(T, 3, 2, 384), (2, 0, 1, 3)).reshape(2, T, 1152)
    dma = pltpu.SemaphoreType.DMA
    out = pl.pallas_call(
        kernel,
        out_shape=jax.ShapeDtypeStruct((2 * T, 1536), BF),
        in_specs=[pl.BlockSpec(memory_space=pltpu.SMEM)] + [any_spec] * 4,
        out_specs=pl.BlockSpec(memory_space=pltpu.VMEM),
        scratch_shapes=[
            pltpu.VMEM((2, 2, T, D), BF),
            pltpu.VMEM((4, 2, 2, T, 1152), BF),
            pltpu.VMEM((15, T, 1536), BF),
            pltpu.VMEM((2, 3, 2 * T, 256), BF),
            pltpu.VMEM((2, 2 * T, 384), BF),
            pltpu.VMEM((2 * T, 1536), BF),
            pltpu.VMEM((2, QT, 1536), BF),
            pltpu.VMEM((2, 2, 2, 4, QT, 1536), BF),
            dma((8,)),
            dma((33,)),
            dma((33,)),
            dma((2, 2, 3, 2)),
            dma((2, 3, 3)),
            dma((2, 2, 3, 3)),
            dma((2, 3, 3)),
        ],
        compiler_params=pltpu.CompilerParams(
            collective_id=0, has_side_effects=True, vmem_limit_bytes=60 * 1024 * 1024
        ),
    )(reach, tokens.reshape(T, D), tangent.reshape(T, D), wq, out_weight.T)
    both = out.reshape(2, 2, 2, 48, 1536)
    return both[0], both[1]


def solution(mesh):
    in_specs = (
        P("tm", "height", None, None),
        P("tm", "height", None, None),
        P("tm", None, "mp"),
        P("mp", "tm"),
        P(None, "mp"),
    )
    out_specs = (P("tm", "height", None, "mp"), P("tm", "height", None, "mp"))
    return jax.shard_map(per_device, mesh=mesh, in_specs=in_specs, out_specs=out_specs, check_vma=False)
```

```python
import jax
import jax.numpy as jnp
from jax import lax
from jax.experimental import pallas as pl
from jax.experimental.pallas import tpu as pltpu
from jax.sharding import PartitionSpec as P

MESH = pl.DeviceIdType.MESH
T = 192
D = 3072
QT = 48
BF = jnp.bfloat16
SENDS = 80
F32 = jnp.float32


def kernel(reach, tok, tan, wq, wot, out0, out1, tk, wk, wqb, kv, qb, hs, hid, wz, wo, lsem, ss, rs, osem, ysem, xsem, csem, hsem):
    tm = lax.axis_index("tm")
    y = lax.axis_index("height")
    mp = lax.axis_index("mp")
    x = lax.div(tm, 4)
    zl = lax.rem(lax.div(tm, 2), 2)
    c = lax.rem(tm, 2)
    z = 2 * mp + zl
    oz = 1 - zl
    df = 1 - 2 * c
    pe = 1 - 2 * lax.rem(x, 2)

    def wrap(i):
        return lax.rem(i + 4, 4)

    def dev(xx, yy, zz, cc):
        return (wrap(xx) * 4 + lax.rem(zz, 2) * 2 + cc, wrap(yy), lax.div(zz, 2))

    sib = dev(x, y, z, 1 - c)
    zin = dev(x, y, 2 * mp + oz, c)
    zout = dev(x, y, 2 * (1 - mp) + oz, c)
    zfar = dev(x, y, 2 * (1 - mp) + zl, c)
    xf, xb, xfar = dev(x + df, y, z, c), dev(x - df, y, z, c), dev(x + 2, y, z, c)
    xpair, xnext = dev(x + pe, y, z, c), dev(x - pe, y, z, c)
    xp = dev(x - df, y, z, 1 - c)
    yf, yb = dev(x, y + df, z, c), dev(x, y - df, z, c)
    yup, ydn = dev(x, y + 1, z, c), dev(x, y - 1, z, c)

    peers = (sib, zin, zout, zfar, xf, xb, xfar, xp, yf, yb)
    barrier = pltpu.get_barrier_semaphore()
    for p in peers:
        pl.semaphore_signal(barrier, inc=1, device_id=p, device_id_type=MESH)

    def rows(yy):
        return pl.ds(pl.multiple_of(QT * wrap(yy), QT), QT)

    yq = rows(y)
    ALL = slice(None)
    holder = lax.div(x, 2) == mp
    me2 = lax.rem(x, 2)

    def chunk_src(n, g, r):
        if n == 3:
            return wq.at[0, r, pl.ds(pl.multiple_of(g * 384, 384), 384)]
        return wq.at[pl.ds(1, 2), r, pl.ds(pl.multiple_of(g * 384 + n * 128, 128), 128)]

    def chunk(n, xx, zz, r):
        return wqb.at[xx, zz, c, r] if n == 3 else wk.at[n, :, xx, zz, c, r]

    def wz_at(q):
        return wz.at[q, zl, :, pl.ds(pl.multiple_of(mp * 768, 768), 768)]

    mine = [pltpu.make_async_copy(chunk_src(n, zl, ALL), chunk(n, x, zl, ALL), lsem.at[n]) for n in range(4)]
    mine += [
        pltpu.make_async_copy(tok, tk.at[0, 0], lsem.at[4]),
        pltpu.make_async_copy(tan, tk.at[0, 1], lsem.at[5]),
        pltpu.make_async_copy(wot.at[yq], wz_at(0), lsem.at[6]),
        pltpu.make_async_copy(wot.at[rows(y + 2)], wz_at(1), lsem.at[7]),
    ]
    for m in mine:
        m.start()
    pl.semaphore_wait(barrier, len(peers))

    started = []

    def put(src, dst, where):
        k = len(started)
        cp = pltpu.make_async_remote_copy(
            src_ref=src, dst_ref=dst, send_sem=ss.at[k], recv_sem=rs.at[k], device_id=where, device_id_type=MESH
        )
        cp.start()
        started.append(cp)
        return cp

    def same(ref, where):
        return put(ref, ref, where)

    def arrived(*copies):
        for cp in copies:
            cp.wait_recv()

    def o_copy(src, dst, where, k):
        return pltpu.make_async_remote_copy(
            src_ref=src, dst_ref=dst, send_sem=osem.at[0, k], recv_sem=osem.at[1, k], device_id=where, device_id_type=MESH
        )

    def wo_z(q, i):
        return o_copy(wot.at[rows(y + 2 * q)], wz_at(q), (zin, zout, zfar)[i], 3 * q + i)

    xl, xr, xo = wrap(x - df), wrap(x + df), wrap(x + 2)
    z_w, o_f, o_b, o_o, x_q, y_f, y_b, y_o = ({} for _ in range(8))
    sibs = [[] for _ in range(4)]

    def own_rows(n):
        src, dst = chunk_src(n, zl, ALL), chunk(n, x, zl, ALL)
        o_f[n], o_b[n] = put(src, dst, xf), put(src, dst, xb)
        sibs[n].append(put(src, dst, sib))

    def share(n, ref):
        sibs[n].append(same(ref, sib))

    def quarter_x(n):
        arrived(z_w[n])
        x_q[n] = [same(chunk(n, x, oz, yq), d) for d in (xf, xb, xfar)]

    def own_relay(n):
        arrived(o_f[n])
        o_o[n] = same(chunk(n, xl, zl, ALL), xf)
        share(n, chunk(n, xl, zl, ALL))

    def quarter_y(n):
        arrived(*x_q[n])
        ref = chunk(n, ALL, oz, yq)
        y_f[n], y_b[n] = same(ref, yf), same(ref, yb)
        share(n, ref)

    def relay_y(n):
        arrived(o_b[n])
        share(n, chunk(n, xr, zl, ALL))
        arrived(y_f[n])
        ref = chunk(n, ALL, oz, rows(y - df))
        y_o[n] = same(ref, yf)
        share(n, ref)

    def last_y(n):
        arrived(y_b[n])
        share(n, chunk(n, ALL, oz, rows(y + df)))
        arrived(o_o[n])
        share(n, chunk(n, xo, zl, ALL))
        arrived(y_o[n])
        share(n, chunk(n, ALL, oz, rows(y + 2)))

    def project(i, tau, h):
        b = 3 * (1 + 2 * tau) + 1
        lhs = tk[i].reshape(2 * T, D)
        rhs = jnp.concatenate([wk[h, j].reshape(D, 128) for j in range(2)], 1)
        r = jnp.dot(lhs, rhs, preferred_element_type=F32).astype(BF)
        for j in range(2):
            at = h * 512 + j * 256
            kv[b, :, at : at + 128] = r[:T, j * 128 : j * 128 + 128]
            kv[b, :, at + 128 : at + 256] = r[T:, j * 128 : j * 128 + 128]

    def project_q(i, tau):
        lhs = tk[i].reshape(2 * T, D)
        r = jnp.dot(lhs, wqb[...].reshape(D, 384), preferred_element_type=F32).astype(BF)
        for h in range(3):
            q, qm = r[:T, h * 128 : h * 128 + 128], r[T:, h * 128 : h * 128 + 128]
            qb[tau, h, :T, :128] = q
            qb[tau, h, :T, 128:] = jnp.zeros_like(q)
            qb[tau, h, T:, :128] = qm
            qb[tau, h, T:, 128:] = q

    def head(b, h):
        return kv.at[b, :, pl.ds(pl.multiple_of(h * 512, 512), 512)]

    def far(sems, idx, src, dst, where):
        return pltpu.make_async_remote_copy(
            src_ref=src,
            dst_ref=dst,
            send_sem=sems.at[(0,) + idx],
            recv_sem=sems.at[(1,) + idx],
            device_id=where,
            device_id_type=MESH,
        )

    def y_copy(tau, h, up):
        s = 3 * (1 + 2 * tau)
        return far(ysem, (tau, h, up), head(s + 1, h), head(s + 2 - 2 * up, h), yup if up else ydn)

    def sib_copy(tau, h, dh):
        s = 1 + 2 * tau
        return far(csem, (tau, h, dh), head(3 * s + dh, h), head(3 * (s - df) + dh, h), sib)

    def x_copy(h, dh):
        return far(xsem, (h, dh), head(3 * (1 + 2 * c) + dh, h), head(12 - 12 * c + dh, h), xp)

    def halo(tau, h, edge):
        y_copy(tau, h, 1).start()
        y_copy(tau, h, 0).start()
        sib_copy(tau, h, 1).start()

        @pl.when(edge)
        def _():
            x_copy(h, 1).start()

    def wo_at(slot, q, zz):
        return wo.at[slot, zz, c, wrap(y + 2 * q)]

    def wo_pair(src, slot, q, zz):
        return o_copy(src, wo_at(slot, q, zz), xpair, 6 + 2 * q + zz)

    def wo_next(q, zz):
        return o_copy(wz.at[q, zz], wo_at(me2, q, zz), xnext, 10 + 2 * q + zz)

    def wo_own(q, zz):
        return pltpu.make_async_copy(wz.at[q, zz], wo_at(me2, q, zz), lsem.at[11 + 2 * q + zz])

    def wo_relay(q, zz):
        @pl.when(jnp.logical_not(holder))
        def _():
            wo_next(q, zz).wait_recv()
            wo_pair(wo_at(1 - me2, q, zz), 1 - me2, q, zz).start()

    def own_tile(h):
        last_y(h)
        arrived(*sibs[h])
        project(0, zl, h)
        halo(zl, h, zl == c)

    for n in range(4):
        z_w[n] = put(chunk_src(n, oz, yq), chunk(n, x, zl, yq), zin)
    own_rows(0)
    for q in range(2):

        @pl.when(holder)
        def _(q=q):
            wo_z(q, 0).start()

        @pl.when(jnp.logical_not(holder))
        def _(q=q):
            wo_z(q, 1).start()
            wo_z(q, 2).start()

    t0 = put(tok, tk.at[1, 0], zin)
    t1 = put(tan, tk.at[1, 1], zout)
    for n in range(4):
        quarter_x(n)
    def own_halo(h, carry):
        for up in range(2):
            y_copy(zl, h, up).wait_recv()
        for dh in (0, 2):
            sib_copy(zl, h, dh).start()

        @pl.when(zl == c)
        def _():
            for dh in (0, 2):
                x_copy(h, dh).start()

        return carry

    def partner_start(h):
        halo(oz, h, zl != c)

    def wo_first(q):
        @pl.when(holder)
        def _():
            for i in range(3):
                wo_z(q, i).wait_recv()
            for zz in range(2):
                wo_next(q, zz).start()
                wo_pair(wz.at[q, zz], me2, q, zz).start()
                wo_own(q, zz).start()

    own_relay(0)
    own_rows(1)
    own_rows(2)
    for n in range(3):
        quarter_y(n)
    relay_y(0)
    own_relay(1)
    relay_y(1)
    for m in mine:
        m.wait()
    wo_first(0)
    own_tile(0)
    own_relay(2)
    own_rows(3)
    wo_first(1)
    relay_y(2)
    own_tile(1)
    own_tile(2)
    wo_relay(0, 0)
    own_relay(3)
    quarter_y(3)
    wo_relay(0, 1)
    own_halo(0, 0)
    relay_y(3)
    arrived(t0, t1)
    for h in range(3):
        project(1, oz, h)

        @pl.when(zl != c)
        def _(h=h):
            partner_start(h)

    wo_relay(1, 0)
    lax.fori_loop(1, 3, own_halo, 0)

    @pl.when(zl == c)
    def _():
        for h in range(3):
            partner_start(h)

    wo_relay(1, 1)
    last_y(3)
    arrived(*sibs[3])
    project_q(0, zl)
    project_q(1, oz)

    def attend(tau, h):
        k = kv[pl.ds(6 * tau, 9), :, pl.ds(pl.multiple_of(h * 512, 256), 256)].reshape(9 * T, 256)
        v = kv[pl.ds(6 * tau, 9), :, pl.ds(pl.multiple_of(h * 512 + 256, 256), 256)].reshape(9 * T, 256)
        both = lax.dot_general(qb[tau, h], k, (((1,), (1,)), ((), ())), preferred_element_type=F32)
        tile = 4 * x + 2 * tau + c
        hid_h = 3 * zl + h
        low = jnp.float32(-1e30)
        zero = jnp.float32(0.0)
        rf, rr = reach[0, hid_h], reach[1, hid_h]
        left = jnp.where((rf >= 1) & (tile > 0), zero, low)
        right = jnp.where((rf >= 1) & (tile < 15), zero, low)
        above = jnp.where((rr >= 1) & (y > 0), zero, low)
        below = jnp.where((rr >= 1) & (y < 3), zero, low)
        col = lax.broadcasted_iota(jnp.int32, (1, 9 * T), 1)
        bias = jnp.where(col < 3 * T, left, jnp.where(col >= 6 * T, right, zero))
        row = col - jnp.where(col < 3 * T, 0, jnp.where(col >= 6 * T, 6 * T, 3 * T))
        bias = bias + jnp.where(row < T, above, jnp.where(row >= 2 * T, below, zero))
        factor = 1.0 / 128**0.5
        s = both[:T] * factor + bias
        e = jnp.exp(s - jnp.max(s, axis=-1, keepdims=True))
        p = e * (1.0 / jnp.sum(e, axis=-1, keepdims=True))
        m = p * (both[T:] * factor)
        shift = jnp.sum(m, axis=-1, keepdims=True)
        lhs = jnp.concatenate([p.astype(BF), m.astype(BF)], 0)
        r = jnp.dot(lhs, v, preferred_element_type=F32)
        o = r[:T, :128]
        om = r[:T, 128:] + r[T:, :128] - o * shift
        at = pl.ds(pl.multiple_of(h * 128, 128), 128)
        hs[tau, :T, at] = o.astype(BF)
        hs[tau, T:, at] = om.astype(BF)

    def hid_copies(tau, h):
        at = pl.ds(pl.multiple_of(h * 128, 128), 128)
        src = hs.at[tau, :, at]
        dst = hid.at[:, pl.ds(pl.multiple_of(z * 384 + h * 128, 128), 128)]
        own = pltpu.make_async_copy(src, dst, lsem.at[8 + h])
        return own, [far(hsem, (i, h), src, dst, d) for i, d in enumerate((zin, zout, zfar))]

    def send_hidden(tau, h):
        own, (a, b, f) = hid_copies(tau, h)

        @pl.when(tau == zl)
        def _():
            own.start()
            f.start()

        @pl.when(tau != zl)
        def _():
            a.start()
            b.start()

    def partner_halo(h):
        for up in range(2):
            y_copy(oz, h, up).wait_recv()

        @pl.when(zl != c)
        def _():
            for dh in (0, 2):
                x_copy(h, dh).start()

        for dh in (0, 2):
            sib_copy(oz, h, dh).start()

    def inner(h):
        for tau in range(2):
            for dh in range(3):
                sib_copy(tau, h, dh).wait_recv()
        attend(1 - c, h)
        send_hidden(1 - c, h)

    def edge(h):
        for dh in range(3):
            x_copy(h, dh).wait_recv()
        attend(c, h)
        send_hidden(c, h)

    def wo_ready(q):
        for zz in range(2):
            wo_pair(wz.at[q, zz], me2, q, zz).wait_recv()

            @pl.when(holder)
            def _(zz=zz):
                wo_own(q, zz).wait()

    partner_halo(0)
    inner(0)
    wo_ready(0)

    def middle(h, carry):
        partner_halo(h)

        @pl.when(h == 2)
        def _():
            for cp in wy:
                cp.start()

        inner(h)
        edge(h - 1)
        return carry

    quarter = wo.at[:, :, c, y]
    wy = [o_copy(quarter, quarter, d, 14 + i) for i, d in enumerate((yf, yb))]
    lax.fori_loop(1, 3, middle, 0)
    o_sib = [same(quarter, sib)]
    edge(2)

    wo_ready(1)
    o_sib.append(same(wo.at[:, :, c, wrap(y + 2)], sib))
    for i, cp in enumerate(wy):
        arrived(cp)
        o_sib.append(same(wo.at[:, :, c, wrap(y - df + 2 * df * i)], sib))
    arrived(*o_sib)

    for h in range(3):
        own, remote = hid_copies(zl, h)
        own.wait()
        for cp in remote:
            cp.wait_recv()

    for a in range(2):
        r = lax.dot_general(
            hid[...], wo[a].reshape(768, 1536), (((1,), (1,)), ((), ())), preferred_element_type=F32
        ).astype(BF)
        for f in range(2):
            for i in range(2):
                at = (2 * f + i) * 48
                out0[f, i, :, a * 768 : a * 768 + 768] = r[at : at + 48]
                out1[f, i, :, a * 768 : a * 768 + 768] = r[T + at : T + at + 48]

    for cp in started + wy:
        cp.wait_send()

    for q in range(2):
        for zz in range(2):
            wo_pair(wz.at[q, zz], me2, q, zz).wait_send()

            @pl.when(holder)
            def _(q=q, zz=zz):
                wo_next(q, zz).wait_send()

        @pl.when(holder)
        def _(q=q):
            wo_z(q, 0).wait_send()

        @pl.when(jnp.logical_not(holder))
        def _(q=q):
            wo_z(q, 1).wait_send()
            wo_z(q, 2).wait_send()

    def drain(h, carry):
        for tau in range(2):
            for up in range(2):
                y_copy(tau, h, up).wait_send()
            for dh in range(3):
                sib_copy(tau, h, dh).wait_send()
        for dh in range(3):
            x_copy(h, dh).wait_send()
        own, remote = hid_copies(zl, h)
        for cp in remote:
            cp.wait_send()
        return carry

    lax.fori_loop(0, 3, drain, 0)


def per_device(tokens, tangent, qkv_weight, out_weight, reach):
    any_spec = pl.BlockSpec(memory_space=pl.ANY)
    vmem = pl.BlockSpec(memory_space=pltpu.VMEM)
    dma = pltpu.SemaphoreType.DMA
    result = jax.ShapeDtypeStruct((2, 2, 48, 1536), BF)
    return pl.pallas_call(
        kernel,
        out_shape=(result, result),
        in_specs=[pl.BlockSpec(memory_space=pltpu.SMEM)] + [any_spec] * 4,
        out_specs=(vmem, vmem),
        scratch_shapes=[
            pltpu.VMEM((2, 2, T, D), BF),
            pltpu.VMEM((3, 2, 4, 2, 2, T, 128), BF),
            pltpu.VMEM((4, 2, 2, T, 384), BF),
            pltpu.VMEM((15, T, 1536), BF),
            pltpu.VMEM((2, 3, 2 * T, 256), BF),
            pltpu.VMEM((2, 2 * T, 384), BF),
            pltpu.VMEM((2 * T, 1536), BF),
            pltpu.VMEM((2, 2, QT, 1536), BF),
            pltpu.VMEM((2, 2, 2, 4, QT, 1536), BF),
            dma((15,)),
            dma((SENDS,)),
            dma((SENDS,)),
            dma((2, 16)),
            dma((2, 2, 3, 2)),
            dma((2, 3, 3)),
            dma((2, 2, 3, 3)),
            dma((2, 3, 3)),
        ],
        compiler_params=pltpu.CompilerParams(
            collective_id=0, has_side_effects=True, vmem_limit_bytes=60 * 1024 * 1024
        ),
    )(reach, tokens.reshape(T, D), tangent.reshape(T, D), jnp.transpose(qkv_weight, (1, 0, 2)), out_weight.T)


def solution(mesh):
    in_specs = (
        P("tm", "height", None, None),
        P("tm", "height", None, None),
        P("tm", None, "mp"),
        P("mp", "tm"),
        P(None, "mp"),
    )
    out_specs = (P("tm", "height", None, "mp"), P("tm", "height", None, "mp"))
    return jax.shard_map(per_device, mesh=mesh, in_specs=in_specs, out_specs=out_specs, check_vma=False)
```

```python
import jax
import jax.numpy as jnp
from jax import lax
from jax.experimental import pallas as pl
from jax.experimental.pallas import tpu as pltpu
from jax.sharding import PartitionSpec as P

MESH = pl.DeviceIdType.MESH
T = 192
D = 3072
QT = 48
BF = jnp.bfloat16
SENDS = 104
F32 = jnp.float32


def kernel(reach, tok, tan, wq, wot, out0, out1, tk, wk, wqb, kv, qb, hs, hid, wz, wo, lsem, ss, rs, osem, ysem, xsem, csem, hsem):
    tm = lax.axis_index("tm")
    y = lax.axis_index("height")
    mp = lax.axis_index("mp")
    x = lax.div(tm, 4)
    zl = lax.rem(lax.div(tm, 2), 2)
    c = lax.rem(tm, 2)
    z = 2 * mp + zl
    oz = 1 - zl
    df = 1 - 2 * c
    pe = 1 - 2 * lax.rem(x, 2)

    def wrap(i):
        return lax.rem(i + 4, 4)

    def dev(xx, yy, zz, cc):
        return (wrap(xx) * 4 + lax.rem(zz, 2) * 2 + cc, wrap(yy), lax.div(zz, 2))

    sib = dev(x, y, z, 1 - c)
    zin = dev(x, y, 2 * mp + oz, c)
    zout = dev(x, y, 2 * (1 - mp) + oz, c)
    zfar = dev(x, y, 2 * (1 - mp) + zl, c)
    xf, xb, xfar = dev(x + df, y, z, c), dev(x - df, y, z, c), dev(x + 2, y, z, c)
    xpair, xnext = dev(x + pe, y, z, c), dev(x - pe, y, z, c)
    xp = dev(x - df, y, z, 1 - c)
    yf, yb = dev(x, y + df, z, c), dev(x, y - df, z, c)
    yup, ydn = dev(x, y + 1, z, c), dev(x, y - 1, z, c)

    peers = (sib, zin, zout, zfar, xf, xb, xfar, xp, yf, yb)
    barrier = pltpu.get_barrier_semaphore()
    for p in peers:
        pl.semaphore_signal(barrier, inc=1, device_id=p, device_id_type=MESH)

    def rows(yy):
        return pl.ds(pl.multiple_of(QT * wrap(yy), QT), QT)

    yq = rows(y)
    ALL = slice(None)
    holder = lax.div(x, 2) == mp
    me2 = lax.rem(x, 2)

    def chunk_src(n, g, r):
        if n == 3:
            return wq.at[0, r, pl.ds(pl.multiple_of(g * 384, 384), 384)]
        return wq.at[pl.ds(1, 2), r, pl.ds(pl.multiple_of(g * 384 + n * 128, 128), 128)]

    def chunk(n, xx, zz, r):
        return wqb.at[xx, zz, c, r] if n == 3 else wk.at[n, :, xx, zz, c, r]

    def wz_at(q):
        return wz.at[q, zl, :, pl.ds(pl.multiple_of(mp * 768, 768), 768)]

    mine = [pltpu.make_async_copy(chunk_src(n, zl, ALL), chunk(n, x, zl, ALL), lsem.at[n]) for n in range(4)]
    mine += [
        pltpu.make_async_copy(tok, tk.at[0, 0], lsem.at[4]),
        pltpu.make_async_copy(tan, tk.at[0, 1], lsem.at[5]),
        pltpu.make_async_copy(wot.at[yq], wz_at(0), lsem.at[6]),
        pltpu.make_async_copy(wot.at[rows(y + 2)], wz_at(1), lsem.at[7]),
    ]
    for m in mine:
        m.start()
    pl.semaphore_wait(barrier, len(peers))

    started = []

    def put(src, dst, where):
        k = len(started)
        cp = pltpu.make_async_remote_copy(
            src_ref=src, dst_ref=dst, send_sem=ss.at[k], recv_sem=rs.at[k], device_id=where, device_id_type=MESH
        )
        cp.start()
        started.append(cp)
        return cp

    def same(ref, where):
        return put(ref, ref, where)

    def arrived(*copies):
        for cp in copies:
            cp.wait_recv()

    def o_copy(src, dst, where, k):
        return pltpu.make_async_remote_copy(
            src_ref=src, dst_ref=dst, send_sem=osem.at[0, k], recv_sem=osem.at[1, k], device_id=where, device_id_type=MESH
        )

    def wo_z(q, i):
        return o_copy(wot.at[rows(y + 2 * q)], wz_at(q), (zin, zout, zfar)[i], 3 * q + i)

    xl, xr, xo = wrap(x - df), wrap(x + df), wrap(x + 2)
    z_w, o_f, o_b, o_o, x_q, y_f, y_b, y_o = ({} for _ in range(8))
    sibs = [[] for _ in range(4)]

    def own_rows(n):
        src, dst = chunk_src(n, zl, ALL), chunk(n, x, zl, ALL)
        o_f[n], o_b[n] = put(src, dst, xf), put(src, dst, xb)
        sibs[n].append(put(src, dst, sib))

    def share(n, ref):
        sibs[n].append(same(ref, sib))

    def quarter_x(n):
        arrived(z_w[n])
        ref = chunk(n, x, oz, yq)
        x_q[n] = [same(ref, d) for d in (xf, xb, xfar)]
        y_f[n], y_b[n] = [same(ref, yf)], [same(ref, yb)]

    def own_relay(n):
        arrived(o_f[n])
        o_o[n] = same(chunk(n, xl, zl, ALL), xf)
        share(n, chunk(n, xl, zl, ALL))

    def quarter_y(n):
        for cp, xx in zip(x_q[n], (xl, xr, xo)):
            arrived(cp)
            ref = chunk(n, xx, oz, yq)
            y_f[n].append(same(ref, yf))
            y_b[n].append(same(ref, yb))
        share(n, chunk(n, ALL, oz, yq))

    def relay_y(n):
        arrived(o_b[n])
        share(n, chunk(n, xr, zl, ALL))
        arrived(*y_f[n])
        ref = chunk(n, ALL, oz, rows(y - df))
        y_o[n] = same(ref, yf)
        share(n, ref)

    def last_y(n):
        arrived(*y_b[n])
        share(n, chunk(n, ALL, oz, rows(y + df)))
        arrived(o_o[n])
        share(n, chunk(n, xo, zl, ALL))
        arrived(y_o[n])
        share(n, chunk(n, ALL, oz, rows(y + 2)))

    def project(i, tau, h):
        b = 3 * (1 + 2 * tau) + 1
        lhs = tk[i].reshape(2 * T, D)
        rhs = jnp.concatenate([wk[h, j].reshape(D, 128) for j in range(2)], 1)
        r = jnp.dot(lhs, rhs, preferred_element_type=F32).astype(BF)
        for j in range(2):
            at = h * 512 + j * 256
            kv[b, :, at : at + 128] = r[:T, j * 128 : j * 128 + 128]
            kv[b, :, at + 128 : at + 256] = r[T:, j * 128 : j * 128 + 128]

    def project_q(i, tau):
        lhs = tk[i].reshape(2 * T, D)
        r = jnp.dot(lhs, wqb[...].reshape(D, 384), preferred_element_type=F32).astype(BF)
        for h in range(3):
            q, qm = r[:T, h * 128 : h * 128 + 128], r[T:, h * 128 : h * 128 + 128]
            qb[tau, h, :T, :128] = q
            qb[tau, h, :T, 128:] = jnp.zeros_like(q)
            qb[tau, h, T:, :128] = qm
            qb[tau, h, T:, 128:] = q

    def head(b, h):
        return kv.at[b, :, pl.ds(pl.multiple_of(h * 512, 512), 512)]

    def far(sems, idx, src, dst, where):
        return pltpu.make_async_remote_copy(
            src_ref=src,
            dst_ref=dst,
            send_sem=sems.at[(0,) + idx],
            recv_sem=sems.at[(1,) + idx],
            device_id=where,
            device_id_type=MESH,
        )

    def y_copy(tau, h, up):
        s = 3 * (1 + 2 * tau)
        return far(ysem, (tau, h, up), head(s + 1, h), head(s + 2 - 2 * up, h), yup if up else ydn)

    def sib_copy(tau, h, dh):
        s = 1 + 2 * tau
        return far(csem, (tau, h, dh), head(3 * s + dh, h), head(3 * (s - df) + dh, h), sib)

    def x_copy(h, dh):
        return far(xsem, (h, dh), head(3 * (1 + 2 * c) + dh, h), head(12 - 12 * c + dh, h), xp)

    def halo(tau, h, edge):
        y_copy(tau, h, 1).start()
        y_copy(tau, h, 0).start()
        sib_copy(tau, h, 1).start()

        @pl.when(edge)
        def _():
            x_copy(h, 1).start()

    def wo_at(slot, q, zz):
        return wo.at[slot, zz, c, wrap(y + 2 * q)]

    def wo_pair(src, slot, q, zz):
        return o_copy(src, wo_at(slot, q, zz), xpair, 6 + 2 * q + zz)

    def wo_next(q, zz):
        return o_copy(wz.at[q, zz], wo_at(me2, q, zz), xnext, 10 + 2 * q + zz)

    def wo_own(q, zz):
        return pltpu.make_async_copy(wz.at[q, zz], wo_at(me2, q, zz), lsem.at[11 + 2 * q + zz])

    def wo_relay(q, zz):
        @pl.when(jnp.logical_not(holder))
        def _():
            wo_next(q, zz).wait_recv()
            wo_pair(wo_at(1 - me2, q, zz), 1 - me2, q, zz).start()

    def own_tile(h):
        arrived(*sibs[h])
        project(0, zl, h)
        halo(zl, h, zl == c)

    for n in range(4):
        z_w[n] = put(chunk_src(n, oz, yq), chunk(n, x, zl, yq), zin)
    own_rows(0)
    for q in range(2):

        @pl.when(holder)
        def _(q=q):
            wo_z(q, 0).start()

        @pl.when(jnp.logical_not(holder))
        def _(q=q):
            wo_z(q, 1).start()
            wo_z(q, 2).start()

    t0 = put(tok, tk.at[1, 0], zin)
    t1 = put(tan, tk.at[1, 1], zout)
    for n in range(4):
        quarter_x(n)
    def own_halo(h, carry):
        for up in range(2):
            y_copy(zl, h, up).wait_recv()
        for dh in (0, 2):
            sib_copy(zl, h, dh).start()

        @pl.when(zl == c)
        def _():
            for dh in (0, 2):
                x_copy(h, dh).start()

        return carry

    def partner_start(h):
        halo(oz, h, zl != c)

    def wo_first(q):
        @pl.when(holder)
        def _():
            for i in range(3):
                wo_z(q, i).wait_recv()
            for zz in range(2):
                wo_next(q, zz).start()
                wo_pair(wz.at[q, zz], me2, q, zz).start()
                wo_own(q, zz).start()

    own_relay(0)
    own_rows(1)
    own_rows(2)
    for n in range(3):
        quarter_y(n)
    relay_y(0)
    own_relay(1)
    relay_y(1)
    last_y(0)
    quarter_y(3)
    own_relay(2)
    own_rows(3)
    relay_y(2)
    for m in mine:
        m.wait()
    wo_first(0)
    own_tile(0)
    last_y(1)
    own_tile(1)
    last_y(2)
    relay_y(3)
    wo_first(1)
    own_tile(2)
    wo_relay(0, 0)
    own_relay(3)
    wo_relay(0, 1)
    own_halo(0, 0)
    arrived(t0, t1)
    for h in range(3):
        project(1, oz, h)

        partner_start(h)

    wo_relay(1, 0)
    lax.fori_loop(1, 3, own_halo, 0)

    wo_relay(1, 1)
    last_y(3)
    arrived(*sibs[3])
    project_q(0, zl)
    project_q(1, oz)

    def attend(tau, h):
        k = kv[pl.ds(6 * tau, 9), :, pl.ds(pl.multiple_of(h * 512, 256), 256)].reshape(9 * T, 256)
        v = kv[pl.ds(6 * tau, 9), :, pl.ds(pl.multiple_of(h * 512 + 256, 256), 256)].reshape(9 * T, 256)
        both = lax.dot_general(qb[tau, h], k, (((1,), (1,)), ((), ())), preferred_element_type=F32)
        tile = 4 * x + 2 * tau + c
        hid_h = 3 * zl + h
        low = jnp.float32(-1e30)
        zero = jnp.float32(0.0)
        rf, rr = reach[0, hid_h], reach[1, hid_h]
        left = jnp.where((rf >= 1) & (tile > 0), zero, low)
        right = jnp.where((rf >= 1) & (tile < 15), zero, low)
        above = jnp.where((rr >= 1) & (y > 0), zero, low)
        below = jnp.where((rr >= 1) & (y < 3), zero, low)
        col = lax.broadcasted_iota(jnp.int32, (1, 9 * T), 1)
        bias = jnp.where(col < 3 * T, left, jnp.where(col >= 6 * T, right, zero))
        row = col - jnp.where(col < 3 * T, 0, jnp.where(col >= 6 * T, 6 * T, 3 * T))
        bias = bias + jnp.where(row < T, above, jnp.where(row >= 2 * T, below, zero))
        factor = 1.0 / 128**0.5
        s = both[:T] * factor + bias
        e = jnp.exp(s - jnp.max(s, axis=-1, keepdims=True))
        p = e * (1.0 / jnp.sum(e, axis=-1, keepdims=True))
        m = p * (both[T:] * factor)
        shift = jnp.sum(m, axis=-1, keepdims=True)
        lhs = jnp.concatenate([p.astype(BF), m.astype(BF)], 0)
        r = jnp.dot(lhs, v, preferred_element_type=F32)
        o = r[:T, :128]
        om = r[:T, 128:] + r[T:, :128] - o * shift
        at = pl.ds(pl.multiple_of(h * 128, 128), 128)
        hs[tau, :T, at] = o.astype(BF)
        hs[tau, T:, at] = om.astype(BF)

    def hid_copies(tau, h):
        at = pl.ds(pl.multiple_of(h * 128, 128), 128)
        src = hs.at[tau, :, at]
        dst = hid.at[:, pl.ds(pl.multiple_of(z * 384 + h * 128, 128), 128)]
        own = pltpu.make_async_copy(src, dst, lsem.at[8 + h])
        return own, [far(hsem, (i, h), src, dst, d) for i, d in enumerate((zin, zout, zfar))]

    def send_hidden(tau, h):
        own, (a, b, f) = hid_copies(tau, h)

        @pl.when(tau == zl)
        def _():
            own.start()
            f.start()

        @pl.when(tau != zl)
        def _():
            a.start()
            b.start()

    def partner_halo(h):
        for up in range(2):
            y_copy(oz, h, up).wait_recv()

        @pl.when(zl != c)
        def _():
            for dh in (0, 2):
                x_copy(h, dh).start()

        for dh in (0, 2):
            sib_copy(oz, h, dh).start()

    def inner(h):
        for tau in range(2):
            for dh in range(3):
                sib_copy(tau, h, dh).wait_recv()
        attend(1 - c, h)
        send_hidden(1 - c, h)

    def edge(h):
        for dh in range(3):
            x_copy(h, dh).wait_recv()
        attend(c, h)
        send_hidden(c, h)

    def wo_ready(q):
        for zz in range(2):
            wo_pair(wz.at[q, zz], me2, q, zz).wait_recv()

            @pl.when(holder)
            def _(zz=zz):
                wo_own(q, zz).wait()

    wo_ready(0)

    quarter = wo.at[:, :, c, y]
    wy = [o_copy(quarter, quarter, d, 14 + i) for i, d in enumerate((yf, yb))]
    partner_halo(0)
    inner(0)
    partner_halo(1)
    inner(1)
    partner_halo(2)
    for cp in wy:
        cp.start()
    edge(0)
    inner(2)
    edge(1)
    o_sib = [same(quarter, sib)]
    edge(2)

    for cp in started:
        cp.wait_send()
    drained = len(started)

    for q in range(2):
        for zz in range(2):
            wo_pair(wz.at[q, zz], me2, q, zz).wait_send()

            @pl.when(holder)
            def _(q=q, zz=zz):
                wo_next(q, zz).wait_send()

        @pl.when(holder)
        def _(q=q):
            wo_z(q, 0).wait_send()

        @pl.when(jnp.logical_not(holder))
        def _(q=q):
            wo_z(q, 1).wait_send()
            wo_z(q, 2).wait_send()

    def drain(h, carry):
        for tau in range(2):
            for up in range(2):
                y_copy(tau, h, up).wait_send()
            for dh in range(3):
                sib_copy(tau, h, dh).wait_send()
        for dh in range(3):
            x_copy(h, dh).wait_send()
        return carry

    lax.fori_loop(0, 3, drain, 0)

    wo_ready(1)
    o_sib.append(same(wo.at[:, :, c, wrap(y + 2)], sib))
    for i, cp in enumerate(wy):
        arrived(cp)
        o_sib.append(same(wo.at[:, :, c, wrap(y - df + 2 * df * i)], sib))
    arrived(*o_sib)

    for h in range(3):
        own, remote = hid_copies(zl, h)
        own.wait()
        for cp in remote:
            cp.wait_recv()

    for a in range(2):
        r = lax.dot_general(
            hid[...], wo[a].reshape(768, 1536), (((1,), (1,)), ((), ())), preferred_element_type=F32
        ).astype(BF)
        for f in range(2):
            for i in range(2):
                at = (2 * f + i) * 48
                out0[f, i, :, a * 768 : a * 768 + 768] = r[at : at + 48]
                out1[f, i, :, a * 768 : a * 768 + 768] = r[T + at : T + at + 48]

    for cp in started[drained:] + wy:
        cp.wait_send()
    for h in range(3):
        for cp in hid_copies(zl, h)[1]:
            cp.wait_send()


def per_device(tokens, tangent, qkv_weight, out_weight, reach):
    any_spec = pl.BlockSpec(memory_space=pl.ANY)
    vmem = pl.BlockSpec(memory_space=pltpu.VMEM)
    dma = pltpu.SemaphoreType.DMA
    return pl.pallas_call(
        kernel,
        out_shape=(pltpu.VMEM((2, 2, 48, 1536), BF),) * 2,
        in_specs=[pl.BlockSpec(memory_space=pltpu.SMEM)] + [any_spec] * 4,
        out_specs=(vmem, vmem),
        scratch_shapes=[
            pltpu.VMEM((2, 2, T, D), BF),
            pltpu.VMEM((3, 2, 4, 2, 2, T, 128), BF),
            pltpu.VMEM((4, 2, 2, T, 384), BF),
            pltpu.VMEM((15, T, 1536), BF),
            pltpu.VMEM((2, 3, 2 * T, 256), BF),
            pltpu.VMEM((2, 2 * T, 384), BF),
            pltpu.VMEM((2 * T, 1536), BF),
            pltpu.VMEM((2, 2, QT, 1536), BF),
            pltpu.VMEM((2, 2, 2, 4, QT, 1536), BF),
            dma((15,)),
            dma((SENDS,)),
            dma((SENDS,)),
            dma((2, 16)),
            dma((2, 2, 3, 2)),
            dma((2, 3, 3)),
            dma((2, 2, 3, 3)),
            dma((2, 3, 3)),
        ],
        compiler_params=pltpu.CompilerParams(
            collective_id=0, has_side_effects=True, vmem_limit_bytes=60 * 1024 * 1024
        ),
    )(reach, tokens.reshape(T, D), tangent.reshape(T, D), jnp.transpose(qkv_weight, (1, 0, 2)), out_weight.T)


def solution(mesh):
    in_specs = (
        P("tm", "height", None, None),
        P("tm", "height", None, None),
        P("tm", None, "mp"),
        P("mp", "tm"),
        P(None, "mp"),
    )
    out_specs = (P("tm", "height", None, "mp"), P("tm", "height", None, "mp"))
    return jax.shard_map(per_device, mesh=mesh, in_specs=in_specs, out_specs=out_specs, check_vma=False)
```

```python
import jax
import jax.numpy as jnp
from jax import lax
from jax.experimental import pallas as pl
from jax.experimental.pallas import tpu as pltpu
from jax.sharding import PartitionSpec as P

MESH = pl.DeviceIdType.MESH
T = 192
D = 3072
QT = 48
BF = jnp.bfloat16
SENDS = 106
F32 = jnp.float32


def kernel(reach, tok, tan, wq, wot, out0, out1, tk, wk, wqb, kv, qb, hs, hid, wz, wo, acc, lsem, ss, rs, osem, ysem, xsem, csem, hsem):
    tm = lax.axis_index("tm")
    y = lax.axis_index("height")
    mp = lax.axis_index("mp")
    x = lax.div(tm, 4)
    zl = lax.rem(lax.div(tm, 2), 2)
    c = lax.rem(tm, 2)
    z = 2 * mp + zl
    oz = 1 - zl
    df = 1 - 2 * c
    pe = 1 - 2 * lax.rem(x, 2)

    def wrap(i):
        return lax.rem(i + 4, 4)

    def dev(xx, yy, zz, cc):
        return (wrap(xx) * 4 + lax.rem(zz, 2) * 2 + cc, wrap(yy), lax.div(zz, 2))

    sib = dev(x, y, z, 1 - c)
    zin = dev(x, y, 2 * mp + oz, c)
    zout = dev(x, y, 2 * (1 - mp) + oz, c)
    zfar = dev(x, y, 2 * (1 - mp) + zl, c)
    xf, xb, xfar = dev(x + df, y, z, c), dev(x - df, y, z, c), dev(x + 2, y, z, c)
    xpair, xnext = dev(x + pe, y, z, c), dev(x - pe, y, z, c)
    xp = dev(x - df, y, z, 1 - c)
    yf, yb = dev(x, y + df, z, c), dev(x, y - df, z, c)
    yup, ydn = dev(x, y + 1, z, c), dev(x, y - 1, z, c)

    peers = (sib, zin, zout, zfar, xf, xb, xfar, xp, yf, yb)
    barrier = pltpu.get_barrier_semaphore()
    for p in peers:
        pl.semaphore_signal(barrier, inc=1, device_id=p, device_id_type=MESH)

    def rows(yy):
        return pl.ds(pl.multiple_of(QT * wrap(yy), QT), QT)

    yq = rows(y)
    ALL = slice(None)
    holder = lax.div(x, 2) == mp
    me2 = lax.rem(x, 2)

    def chunk_src(n, g, r):
        if n == 3:
            return wq.at[0, r, pl.ds(pl.multiple_of(g * 384, 384), 384)]
        return wq.at[pl.ds(1, 2), r, pl.ds(pl.multiple_of(g * 384 + n * 128, 128), 128)]

    def chunk(n, xx, zz, r):
        return wqb.at[xx, zz, c, r] if n == 3 else wk.at[n, :, xx, zz, c, r]

    def wz_at(q):
        return wz.at[q, zl, :, pl.ds(pl.multiple_of(mp * 768, 768), 768)]

    mine = [pltpu.make_async_copy(chunk_src(n, zl, ALL), chunk(n, x, zl, ALL), lsem.at[n]) for n in range(4)]
    mine += [
        pltpu.make_async_copy(tok, tk.at[0, 0], lsem.at[4]),
        pltpu.make_async_copy(tan, tk.at[0, 1], lsem.at[5]),
        pltpu.make_async_copy(wot.at[yq], wz_at(0), lsem.at[6]),
        pltpu.make_async_copy(wot.at[rows(y + 2)], wz_at(1), lsem.at[7]),
    ]
    for m in mine:
        m.start()
    pl.semaphore_wait(barrier, len(peers))

    started = []

    def put(src, dst, where):
        k = len(started)
        cp = pltpu.make_async_remote_copy(
            src_ref=src, dst_ref=dst, send_sem=ss.at[k], recv_sem=rs.at[k], device_id=where, device_id_type=MESH
        )
        cp.start()
        started.append(cp)
        return cp

    def same(ref, where):
        return put(ref, ref, where)

    def arrived(*copies):
        for cp in copies:
            cp.wait_recv()

    def o_copy(src, dst, where, k):
        return pltpu.make_async_remote_copy(
            src_ref=src, dst_ref=dst, send_sem=osem.at[0, k], recv_sem=osem.at[1, k], device_id=where, device_id_type=MESH
        )

    def wo_z(q, i):
        return o_copy(wot.at[rows(y + 2 * q)], wz_at(q), (zin, zout, zfar)[i], 3 * q + i)

    xl, xr, xo = wrap(x - df), wrap(x + df), wrap(x + 2)
    z_w, o_f, o_b, o_o, x_q, y_f, y_b, y_o = ({} for _ in range(8))
    sibs = [[] for _ in range(4)]

    def own_rows(n):
        src, dst = chunk_src(n, zl, ALL), chunk(n, x, zl, ALL)
        o_f[n], o_b[n] = put(src, dst, xf), put(src, dst, xb)
        sibs[n].append(put(src, dst, sib))

    def share(n, ref):
        sibs[n].append(same(ref, sib))

    def quarter_x(n):
        arrived(z_w[n])
        ref = chunk(n, x, oz, yq)
        x_q[n] = [same(ref, d) for d in (xf, xb, xfar)]
        y_f[n], y_b[n] = [same(ref, yf)], [same(ref, yb)]

    def own_relay(n):
        arrived(o_f[n])
        o_o[n] = same(chunk(n, xl, zl, ALL), xf)
        share(n, chunk(n, xl, zl, ALL))

    def quarter_y(n):
        for cp, xx in zip(x_q[n], (xl, xr, xo)):
            arrived(cp)
            ref = chunk(n, xx, oz, yq)
            y_f[n].append(same(ref, yf))
            y_b[n].append(same(ref, yb))
        share(n, chunk(n, ALL, oz, yq))

    def relay_y(n):
        arrived(o_b[n])
        share(n, chunk(n, xr, zl, ALL))
        arrived(*y_f[n])
        ref = chunk(n, ALL, oz, rows(y - df))
        y_o[n] = same(ref, yf)
        share(n, ref)

    def last_y(n):
        arrived(*y_b[n])
        share(n, chunk(n, ALL, oz, rows(y + df)))
        arrived(o_o[n])
        share(n, chunk(n, xo, zl, ALL))
        arrived(y_o[n])
        share(n, chunk(n, ALL, oz, rows(y + 2)))

    def project(i, tau, h):
        b = 3 * (1 + 2 * tau) + 1
        lhs = tk[i].reshape(2 * T, D)
        rhs = jnp.concatenate([wk[h, j].reshape(D, 128) for j in range(2)], 1)
        r = jnp.dot(lhs, rhs, preferred_element_type=F32).astype(BF)
        for j in range(2):
            at = h * 512 + j * 256
            kv[b, :, at : at + 128] = r[:T, j * 128 : j * 128 + 128]
            kv[b, :, at + 128 : at + 256] = r[T:, j * 128 : j * 128 + 128]

    def project_q(i, tau):
        lhs = tk[i].reshape(2 * T, D)
        r = jnp.dot(lhs, wqb[...].reshape(D, 384), preferred_element_type=F32).astype(BF)
        for h in range(3):
            q, qm = r[:T, h * 128 : h * 128 + 128], r[T:, h * 128 : h * 128 + 128]
            qb[tau, h, :T, :128] = q
            qb[tau, h, :T, 128:] = jnp.zeros_like(q)
            qb[tau, h, T:, :128] = qm
            qb[tau, h, T:, 128:] = q

    def head(b, h):
        return kv.at[b, :, pl.ds(pl.multiple_of(h * 512, 512), 512)]

    def far(sems, idx, src, dst, where):
        return pltpu.make_async_remote_copy(
            src_ref=src,
            dst_ref=dst,
            send_sem=sems.at[(0,) + idx],
            recv_sem=sems.at[(1,) + idx],
            device_id=where,
            device_id_type=MESH,
        )

    def y_copy(tau, h, up):
        s = 3 * (1 + 2 * tau)
        return far(ysem, (tau, h, up), head(s + 1, h), head(s + 2 - 2 * up, h), yup if up else ydn)

    def sib_copy(tau, h, dh):
        s = 1 + 2 * tau
        return far(csem, (tau, h, dh), head(3 * s + dh, h), head(3 * (s - df) + dh, h), sib)

    def x_copy(h, dh):
        return far(xsem, (h, dh), head(3 * (1 + 2 * c) + dh, h), head(12 - 12 * c + dh, h), xp)

    def halo(tau, h, edge):
        y_copy(tau, h, 1).start()
        y_copy(tau, h, 0).start()
        sib_copy(tau, h, 1).start()

        @pl.when(edge)
        def _():
            x_copy(h, 1).start()

    def wo_at(slot, q, zz):
        return wo.at[slot, zz, c, wrap(y + 2 * q)]

    def wo_pair(src, slot, q, zz):
        return o_copy(src, wo_at(slot, q, zz), xpair, 6 + 2 * q + zz)

    def wo_next(q, zz):
        return o_copy(wz.at[q, zz], wo_at(me2, q, zz), xnext, 10 + 2 * q + zz)

    def wo_own(q, zz):
        return pltpu.make_async_copy(wz.at[q, zz], wo_at(me2, q, zz), lsem.at[11 + 2 * q + zz])

    def wo_relay(q, zz):
        @pl.when(jnp.logical_not(holder))
        def _():
            wo_next(q, zz).wait_recv()
            wo_pair(wo_at(1 - me2, q, zz), 1 - me2, q, zz).start()

    def own_tile(h):
        arrived(*sibs[h])
        project(0, zl, h)
        halo(zl, h, zl == c)

    for n in range(4):
        z_w[n] = put(chunk_src(n, oz, yq), chunk(n, x, zl, yq), zin)
    own_rows(0)
    for q in range(2):

        @pl.when(holder)
        def _(q=q):
            wo_z(q, 0).start()

        @pl.when(jnp.logical_not(holder))
        def _(q=q):
            wo_z(q, 1).start()
            wo_z(q, 2).start()

    t0 = put(tok, tk.at[1, 0], zin)
    t1 = put(tan, tk.at[1, 1], zout)
    for n in range(4):
        quarter_x(n)
    def own_halo(h, carry):
        for up in range(2):
            y_copy(zl, h, up).wait_recv()
        for dh in (0, 2):
            sib_copy(zl, h, dh).start()

        @pl.when(zl == c)
        def _():
            for dh in (0, 2):
                x_copy(h, dh).start()

        return carry

    def partner_start(h):
        halo(oz, h, zl != c)

    def wo_first(q):
        @pl.when(holder)
        def _():
            for i in range(3):
                wo_z(q, i).wait_recv()
            for zz in range(2):
                wo_next(q, zz).start()
                wo_pair(wz.at[q, zz], me2, q, zz).start()
                wo_own(q, zz).start()

    own_relay(0)
    own_rows(1)
    own_rows(2)
    for n in range(3):
        quarter_y(n)
    relay_y(0)
    own_relay(1)
    relay_y(1)
    last_y(0)
    quarter_y(3)
    own_relay(2)
    own_rows(3)
    relay_y(2)
    for m in mine:
        m.wait()
    wo_first(0)
    own_tile(0)
    last_y(1)
    own_tile(1)
    last_y(2)
    relay_y(3)
    wo_first(1)
    own_tile(2)
    wo_relay(0, 0)
    own_relay(3)
    wo_relay(0, 1)
    own_halo(0, 0)
    arrived(t0, t1)
    for h in range(3):
        project(1, oz, h)

        partner_start(h)

    wo_relay(1, 0)
    lax.fori_loop(1, 3, own_halo, 0)

    wo_relay(1, 1)
    last_y(3)
    arrived(*sibs[3])
    project_q(0, zl)
    project_q(1, oz)

    def attend(tau, h):
        k = kv[pl.ds(6 * tau, 9), :, pl.ds(pl.multiple_of(h * 512, 256), 256)].reshape(9 * T, 256)
        v = kv[pl.ds(6 * tau, 9), :, pl.ds(pl.multiple_of(h * 512 + 256, 256), 256)].reshape(9 * T, 256)
        both = lax.dot_general(qb[tau, h], k, (((1,), (1,)), ((), ())), preferred_element_type=F32)
        tile = 4 * x + 2 * tau + c
        hid_h = 3 * zl + h
        low = jnp.float32(-1e30)
        zero = jnp.float32(0.0)
        rf, rr = reach[0, hid_h], reach[1, hid_h]
        left = jnp.where((rf >= 1) & (tile > 0), zero, low)
        right = jnp.where((rf >= 1) & (tile < 15), zero, low)
        above = jnp.where((rr >= 1) & (y > 0), zero, low)
        below = jnp.where((rr >= 1) & (y < 3), zero, low)
        col = lax.broadcasted_iota(jnp.int32, (1, 9 * T), 1)
        bias = jnp.where(col < 3 * T, left, jnp.where(col >= 6 * T, right, zero))
        row = col - jnp.where(col < 3 * T, 0, jnp.where(col >= 6 * T, 6 * T, 3 * T))
        bias = bias + jnp.where(row < T, above, jnp.where(row >= 2 * T, below, zero))
        factor = 1.0 / 128**0.5
        s = both[:T] * factor + bias
        e = jnp.exp(s - jnp.max(s, axis=-1, keepdims=True))
        p = e * (1.0 / jnp.sum(e, axis=-1, keepdims=True))
        m = p * (both[T:] * factor)
        shift = jnp.sum(m, axis=-1, keepdims=True)
        lhs = jnp.concatenate([p.astype(BF), m.astype(BF)], 0)
        r = jnp.dot(lhs, v, preferred_element_type=F32)
        o = r[:T, :128]
        om = r[:T, 128:] + r[T:, :128] - o * shift
        at = pl.ds(pl.multiple_of(h * 128, 128), 128)
        hs[tau, :T, at] = o.astype(BF)
        hs[tau, T:, at] = om.astype(BF)

    def hid_copies(tau, h):
        at = pl.ds(pl.multiple_of(h * 128, 128), 128)
        src = hs.at[tau, :, at]
        dst = hid.at[:, pl.ds(pl.multiple_of(z * 384 + h * 128, 128), 128)]
        own = pltpu.make_async_copy(src, dst, lsem.at[8 + h])
        return own, [far(hsem, (i, h), src, dst, d) for i, d in enumerate((zin, zout, zfar))]

    def send_hidden(tau, h):
        own, (a, b, f) = hid_copies(tau, h)

        @pl.when(tau == zl)
        def _():
            own.start()
            f.start()

        @pl.when(tau != zl)
        def _():
            a.start()
            b.start()

    def partner_halo(h):
        for up in range(2):
            y_copy(oz, h, up).wait_recv()

        @pl.when(zl != c)
        def _():
            for dh in (0, 2):
                x_copy(h, dh).start()

        for dh in (0, 2):
            sib_copy(oz, h, dh).start()

    def inner(h):
        for tau in range(2):
            for dh in range(3):
                sib_copy(tau, h, dh).wait_recv()
        attend(1 - c, h)
        send_hidden(1 - c, h)

    def edge(h):
        for dh in range(3):
            x_copy(h, dh).wait_recv()
        attend(c, h)
        send_hidden(c, h)

    def wo_ready(q):
        for zz in range(2):
            wo_pair(wz.at[q, zz], me2, q, zz).wait_recv()

            @pl.when(holder)
            def _(zz=zz):
                wo_own(q, zz).wait()

    wo_ready(0)

    def wo_y(slot, i):
        ref = wo.at[slot, :, c, y]
        return o_copy(ref, ref, (yf, yb)[i], 14 + 2 * slot + i)

    wy = [wo_y(slot, i) for slot in range(2) for i in range(2)]
    for cp in wy:
        cp.start()
    o_sib = [[same(wo.at[slot, :, c, y], sib)] for slot in range(2)]
    partner_halo(0)
    inner(0)
    partner_halo(1)
    inner(1)
    partner_halo(2)
    edge(0)
    inner(2)
    edge(1)
    edge(2)

    for cp in started:
        cp.wait_send()
    drained = len(started)

    for q in range(2):
        for zz in range(2):
            wo_pair(wz.at[q, zz], me2, q, zz).wait_send()

            @pl.when(holder)
            def _(q=q, zz=zz):
                wo_next(q, zz).wait_send()

        @pl.when(holder)
        def _(q=q):
            wo_z(q, 0).wait_send()

        @pl.when(jnp.logical_not(holder))
        def _(q=q):
            wo_z(q, 1).wait_send()
            wo_z(q, 2).wait_send()

    def drain(h, carry):
        for tau in range(2):
            for up in range(2):
                y_copy(tau, h, up).wait_send()
            for dh in range(3):
                sib_copy(tau, h, dh).wait_send()
        for dh in range(3):
            x_copy(h, dh).wait_send()
        return carry

    lax.fori_loop(0, 3, drain, 0)

    wo_ready(1)
    for slot in range(2):
        o_sib[slot].append(same(wo.at[slot, :, c, wrap(y + 2)], sib))

    def hidden(h):
        own, remote = hid_copies(zl, h)
        own.wait()
        arrived(*remote)

    def mix(a, lo, n):
        lhs = jnp.concatenate([hid[:, i * 384 + lo : i * 384 + lo + n] for i in range(4)], 1)
        rhs = wo[a].reshape(768, 1536)
        rhs = jnp.concatenate([rhs[:, i * 384 + lo : i * 384 + lo + n] for i in range(4)], 1)
        return lax.dot_general(lhs, rhs, (((1,), (1,)), ((), ())), preferred_element_type=F32)

    hidden(0)
    hidden(1)
    for a in range(2):
        for i in range(2):
            arrived(wy[2 * a + i])
            o_sib[a].append(same(wo.at[a, :, c, wrap(y - df + 2 * df * i)], sib))
        arrived(*o_sib[a])
        acc[a] = mix(a, 0, 256)
    hidden(2)
    for a in range(2):
        r = (acc[a] + mix(a, 256, 128)).astype(BF)
        for f in range(2):
            for i in range(2):
                at = (2 * f + i) * 48
                out0[f, i, :, a * 768 : a * 768 + 768] = r[at : at + 48]
                out1[f, i, :, a * 768 : a * 768 + 768] = r[T + at : T + at + 48]

    for cp in started[drained:] + wy:
        cp.wait_send()
    for h in range(3):
        for cp in hid_copies(zl, h)[1]:
            cp.wait_send()


def per_device(tokens, tangent, qkv_weight, out_weight, reach):
    any_spec = pl.BlockSpec(memory_space=pl.ANY)
    vmem = pl.BlockSpec(memory_space=pltpu.VMEM)
    dma = pltpu.SemaphoreType.DMA
    return pl.pallas_call(
        kernel,
        out_shape=(pltpu.VMEM((2, 2, 48, 1536), BF),) * 2,
        in_specs=[pl.BlockSpec(memory_space=pltpu.SMEM)] + [any_spec] * 4,
        out_specs=(vmem, vmem),
        scratch_shapes=[
            pltpu.VMEM((2, 2, T, D), BF),
            pltpu.VMEM((3, 2, 4, 2, 2, T, 128), BF),
            pltpu.VMEM((4, 2, 2, T, 384), BF),
            pltpu.VMEM((15, T, 1536), BF),
            pltpu.VMEM((2, 3, 2 * T, 256), BF),
            pltpu.VMEM((2, 2 * T, 384), BF),
            pltpu.VMEM((2 * T, 1536), BF),
            pltpu.VMEM((2, 2, QT, 1536), BF),
            pltpu.VMEM((2, 2, 2, 4, QT, 1536), BF),
            pltpu.VMEM((2, 2 * T, 768), F32),
            dma((15,)),
            dma((SENDS,)),
            dma((SENDS,)),
            dma((2, 18)),
            dma((2, 2, 3, 2)),
            dma((2, 3, 3)),
            dma((2, 2, 3, 3)),
            dma((2, 3, 3)),
        ],
        compiler_params=pltpu.CompilerParams(
            collective_id=0, has_side_effects=True, vmem_limit_bytes=60 * 1024 * 1024
        ),
    )(reach, tokens.reshape(T, D), tangent.reshape(T, D), jnp.transpose(qkv_weight, (1, 0, 2)), out_weight.T)


def solution(mesh):
    in_specs = (
        P("tm", "height", None, None),
        P("tm", "height", None, None),
        P("tm", None, "mp"),
        P("mp", "tm"),
        P(None, "mp"),
    )
    out_specs = (P("tm", "height", None, "mp"), P("tm", "height", None, "mp"))
    return jax.shard_map(per_device, mesh=mesh, in_specs=in_specs, out_specs=out_specs, check_vma=False)
```

```python
import jax
import jax.numpy as jnp
from jax import lax
from jax.experimental import pallas as pl
from jax.experimental.pallas import tpu as pltpu
from jax.sharding import PartitionSpec as P

MESH = pl.DeviceIdType.MESH
T = 192
D = 3072
QT = 48
BF = jnp.bfloat16
SENDS = 106
F32 = jnp.float32


def kernel(reach, tok, tan, wq, wot, out, tk, wk, wqb, kv, qb, hs, hid, wz, wo, acc, lsem, ss, rs, osem, ysem, xsem, csem, hsem):
    tm = lax.axis_index("tm")
    y = lax.axis_index("height")
    mp = lax.axis_index("mp")
    x = lax.div(tm, 4)
    zl = lax.rem(lax.div(tm, 2), 2)
    c = lax.rem(tm, 2)
    z = 2 * mp + zl
    oz = 1 - zl
    df = 1 - 2 * c
    pe = 1 - 2 * lax.rem(x, 2)

    def wrap(i):
        return lax.rem(i + 4, 4)

    def dev(xx, yy, zz, cc):
        return (wrap(xx) * 4 + lax.rem(zz, 2) * 2 + cc, wrap(yy), lax.div(zz, 2))

    sib = dev(x, y, z, 1 - c)
    zin = dev(x, y, 2 * mp + oz, c)
    zout = dev(x, y, 2 * (1 - mp) + oz, c)
    zfar = dev(x, y, 2 * (1 - mp) + zl, c)
    xf, xb, xfar = dev(x + df, y, z, c), dev(x - df, y, z, c), dev(x + 2, y, z, c)
    xpair, xnext = dev(x + pe, y, z, c), dev(x - pe, y, z, c)
    xp = dev(x - df, y, z, 1 - c)
    yf, yb = dev(x, y + df, z, c), dev(x, y - df, z, c)
    yup, ydn = dev(x, y + 1, z, c), dev(x, y - 1, z, c)

    peers = (sib, zin, zout, zfar, xf, xb, xfar, xp, yf, yb)
    barrier = pltpu.get_barrier_semaphore()
    for p in peers:
        pl.semaphore_signal(barrier, inc=1, device_id=p, device_id_type=MESH)

    def rows(yy):
        return pl.ds(pl.multiple_of(QT * wrap(yy), QT), QT)

    yq = rows(y)
    ALL = slice(None)
    holder = lax.div(x, 2) == mp
    me2 = lax.rem(x, 2)

    def chunk_src(n, g, r):
        if n == 3:
            return wq.at[0, r, pl.ds(pl.multiple_of(g * 384, 384), 384)]
        return wq.at[pl.ds(1, 2), r, pl.ds(pl.multiple_of(g * 384 + n * 128, 128), 128)]

    def chunk(n, xx, zz, r):
        return wqb.at[xx, zz, c, r] if n == 3 else wk.at[n, :, xx, zz, c, r]

    def wz_at(q):
        return wz.at[q, zl, :, pl.ds(pl.multiple_of(mp * 768, 768), 768)]

    mine = [pltpu.make_async_copy(chunk_src(n, zl, ALL), chunk(n, x, zl, ALL), lsem.at[n]) for n in range(4)]
    mine += [
        pltpu.make_async_copy(tok, tk.at[0, 0], lsem.at[4]),
        pltpu.make_async_copy(tan, tk.at[0, 1], lsem.at[5]),
        pltpu.make_async_copy(wot.at[yq], wz_at(0), lsem.at[6]),
        pltpu.make_async_copy(wot.at[rows(y + 2)], wz_at(1), lsem.at[7]),
    ]
    for m in mine:
        m.start()
    pl.semaphore_wait(barrier, len(peers))

    started = []

    def put(src, dst, where):
        k = len(started)
        cp = pltpu.make_async_remote_copy(
            src_ref=src, dst_ref=dst, send_sem=ss.at[k], recv_sem=rs.at[k], device_id=where, device_id_type=MESH
        )
        cp.start()
        started.append(cp)
        return cp

    def same(ref, where):
        return put(ref, ref, where)

    def arrived(*copies):
        for cp in copies:
            cp.wait_recv()

    def o_copy(src, dst, where, k):
        return pltpu.make_async_remote_copy(
            src_ref=src, dst_ref=dst, send_sem=osem.at[0, k], recv_sem=osem.at[1, k], device_id=where, device_id_type=MESH
        )

    def wo_z(q, i):
        return o_copy(wot.at[rows(y + 2 * q)], wz_at(q), (zin, zout, zfar)[i], 3 * q + i)

    xl, xr, xo = wrap(x - df), wrap(x + df), wrap(x + 2)
    z_w, o_f, o_b, o_o, x_q, y_f, y_b, y_o = ({} for _ in range(8))
    sibs = [[] for _ in range(4)]

    def own_rows(n):
        src, dst = chunk_src(n, zl, ALL), chunk(n, x, zl, ALL)
        o_f[n], o_b[n] = put(src, dst, xf), put(src, dst, xb)
        sibs[n].append(put(src, dst, sib))

    def share(n, ref):
        sibs[n].append(same(ref, sib))

    def quarter_x(n):
        arrived(z_w[n])
        ref = chunk(n, x, oz, yq)
        x_q[n] = [same(ref, d) for d in (xf, xb, xfar)]
        y_f[n], y_b[n] = [same(ref, yf)], [same(ref, yb)]

    def own_relay(n):
        arrived(o_f[n])
        o_o[n] = same(chunk(n, xl, zl, ALL), xf)
        share(n, chunk(n, xl, zl, ALL))

    def quarter_y(n):
        for cp, xx in zip(x_q[n], (xl, xr, xo)):
            arrived(cp)
            ref = chunk(n, xx, oz, yq)
            y_f[n].append(same(ref, yf))
            y_b[n].append(same(ref, yb))
        share(n, chunk(n, ALL, oz, yq))

    def relay_y(n):
        arrived(o_b[n])
        share(n, chunk(n, xr, zl, ALL))
        arrived(*y_f[n])
        ref = chunk(n, ALL, oz, rows(y - df))
        y_o[n] = same(ref, yf)
        share(n, ref)

    def last_y(n):
        arrived(*y_b[n])
        share(n, chunk(n, ALL, oz, rows(y + df)))
        arrived(o_o[n])
        share(n, chunk(n, xo, zl, ALL))
        arrived(y_o[n])
        share(n, chunk(n, ALL, oz, rows(y + 2)))

    def project(i, tau, h):
        b = 3 * (1 + 2 * tau) + 1
        lhs = tk[i].reshape(2 * T, D)
        rhs = jnp.concatenate([wk[h, j].reshape(D, 128) for j in range(2)], 1)
        r = jnp.dot(lhs, rhs, preferred_element_type=F32).astype(BF)
        for j in range(2):
            at = h * 512 + j * 256
            kv[b, :, at : at + 128] = r[:T, j * 128 : j * 128 + 128]
            kv[b, :, at + 128 : at + 256] = r[T:, j * 128 : j * 128 + 128]

    def project_q(i, tau):
        lhs = tk[i].reshape(2 * T, D)
        r = jnp.dot(lhs, wqb[...].reshape(D, 384), preferred_element_type=F32).astype(BF)
        for h in range(3):
            q, qm = r[:T, h * 128 : h * 128 + 128], r[T:, h * 128 : h * 128 + 128]
            qb[tau, h, :T, :128] = q
            qb[tau, h, :T, 128:] = jnp.zeros_like(q)
            qb[tau, h, T:, :128] = qm
            qb[tau, h, T:, 128:] = q

    def head(b, h):
        return kv.at[b, :, pl.ds(pl.multiple_of(h * 512, 512), 512)]

    def far(sems, idx, src, dst, where):
        return pltpu.make_async_remote_copy(
            src_ref=src,
            dst_ref=dst,
            send_sem=sems.at[(0,) + idx],
            recv_sem=sems.at[(1,) + idx],
            device_id=where,
            device_id_type=MESH,
        )

    def y_copy(tau, h, up):
        s = 3 * (1 + 2 * tau)
        return far(ysem, (tau, h, up), head(s + 1, h), head(s + 2 - 2 * up, h), yup if up else ydn)

    def sib_copy(tau, h, dh):
        s = 1 + 2 * tau
        return far(csem, (tau, h, dh), head(3 * s + dh, h), head(3 * (s - df) + dh, h), sib)

    def x_copy(h, dh):
        return far(xsem, (h, dh), head(3 * (1 + 2 * c) + dh, h), head(12 - 12 * c + dh, h), xp)

    def halo(tau, h, edge):
        y_copy(tau, h, 1).start()
        y_copy(tau, h, 0).start()
        sib_copy(tau, h, 1).start()

        @pl.when(edge)
        def _():
            x_copy(h, 1).start()

    def wo_at(slot, q, zz):
        return wo.at[slot, zz, c, wrap(y + 2 * q)]

    def wo_pair(src, slot, q, zz):
        return o_copy(src, wo_at(slot, q, zz), xpair, 6 + 2 * q + zz)

    def wo_next(q, zz):
        return o_copy(wz.at[q, zz], wo_at(me2, q, zz), xnext, 10 + 2 * q + zz)

    def wo_own(q, zz):
        return pltpu.make_async_copy(wz.at[q, zz], wo_at(me2, q, zz), lsem.at[11 + 2 * q + zz])

    def wo_relay(q, zz):
        @pl.when(jnp.logical_not(holder))
        def _():
            wo_next(q, zz).wait_recv()
            wo_pair(wo_at(1 - me2, q, zz), 1 - me2, q, zz).start()

    def own_tile(h):
        arrived(*sibs[h])
        project(0, zl, h)
        halo(zl, h, zl == c)

    for n in range(4):
        z_w[n] = put(chunk_src(n, oz, yq), chunk(n, x, zl, yq), zin)
    own_rows(0)
    for q in range(2):

        @pl.when(holder)
        def _(q=q):
            wo_z(q, 0).start()

        @pl.when(jnp.logical_not(holder))
        def _(q=q):
            wo_z(q, 1).start()
            wo_z(q, 2).start()

    t0 = put(tok, tk.at[1, 0], zin)
    t1 = put(tan, tk.at[1, 1], zout)
    for n in range(4):
        quarter_x(n)
    def own_halo(h, carry):
        for up in range(2):
            y_copy(zl, h, up).wait_recv()
        for dh in (0, 2):
            sib_copy(zl, h, dh).start()

        @pl.when(zl == c)
        def _():
            for dh in (0, 2):
                x_copy(h, dh).start()

        return carry

    def partner_start(h):
        halo(oz, h, zl != c)

    def wo_first(q):
        @pl.when(holder)
        def _():
            for i in range(3):
                wo_z(q, i).wait_recv()
            for zz in range(2):
                wo_next(q, zz).start()
                wo_pair(wz.at[q, zz], me2, q, zz).start()
                wo_own(q, zz).start()

    own_relay(0)
    own_rows(1)
    own_rows(2)
    for n in range(3):
        quarter_y(n)
    relay_y(0)
    own_relay(1)
    relay_y(1)
    last_y(0)
    quarter_y(3)
    own_relay(2)
    own_rows(3)
    relay_y(2)
    for m in mine:
        m.wait()
    wo_first(0)
    wo_first(1)
    own_tile(0)
    last_y(1)
    own_tile(1)
    last_y(2)
    relay_y(3)
    own_tile(2)
    wo_relay(0, 0)
    own_relay(3)
    wo_relay(0, 1)
    own_halo(0, 0)
    arrived(t0, t1)
    for h in range(3):
        project(1, oz, h)

        partner_start(h)

    wo_relay(1, 0)
    lax.fori_loop(1, 3, own_halo, 0)

    wo_relay(1, 1)
    last_y(3)
    arrived(*sibs[3])
    project_q(0, zl)
    project_q(1, oz)

    def attend(tau, h):
        k = kv[pl.ds(6 * tau, 9), :, pl.ds(pl.multiple_of(h * 512, 256), 256)].reshape(9 * T, 256)
        v = kv[pl.ds(6 * tau, 9), :, pl.ds(pl.multiple_of(h * 512 + 256, 256), 256)].reshape(9 * T, 256)
        both = lax.dot_general(qb[tau, h], k, (((1,), (1,)), ((), ())), preferred_element_type=F32)
        tile = 4 * x + 2 * tau + c
        hid_h = 3 * zl + h
        low = jnp.float32(-1e30)
        zero = jnp.float32(0.0)
        rf, rr = reach[0, hid_h], reach[1, hid_h]
        left = jnp.where((rf >= 1) & (tile > 0), zero, low)
        right = jnp.where((rf >= 1) & (tile < 15), zero, low)
        above = jnp.where((rr >= 1) & (y > 0), zero, low)
        below = jnp.where((rr >= 1) & (y < 3), zero, low)
        col = lax.broadcasted_iota(jnp.int32, (1, 9 * T), 1)
        bias = jnp.where(col < 3 * T, left, jnp.where(col >= 6 * T, right, zero))
        row = col - jnp.where(col < 3 * T, 0, jnp.where(col >= 6 * T, 6 * T, 3 * T))
        bias = bias + jnp.where(row < T, above, jnp.where(row >= 2 * T, below, zero))
        factor = 1.0 / 128**0.5
        s = both[:T] * factor + bias
        e = jnp.exp(s - jnp.max(s, axis=-1, keepdims=True))
        p = e * (1.0 / jnp.sum(e, axis=-1, keepdims=True))
        m = p * (both[T:] * factor)
        shift = jnp.sum(m, axis=-1, keepdims=True)
        lhs = jnp.concatenate([p.astype(BF), m.astype(BF)], 0)
        r = jnp.dot(lhs, v, preferred_element_type=F32)
        o = r[:T, :128]
        om = r[:T, 128:] + r[T:, :128] - o * shift
        at = pl.ds(pl.multiple_of(h * 128, 128), 128)
        hs[tau, :T, at] = o.astype(BF)
        hs[tau, T:, at] = om.astype(BF)

    def hid_copies(tau, h):
        at = pl.ds(pl.multiple_of(h * 128, 128), 128)
        src = hs.at[tau, :, at]
        dst = hid.at[:, pl.ds(pl.multiple_of(z * 384 + h * 128, 128), 128)]
        own = pltpu.make_async_copy(src, dst, lsem.at[8 + h])
        return own, [far(hsem, (i, h), src, dst, d) for i, d in enumerate((zin, zout, zfar))]

    def send_hidden(tau, h):
        own, (a, b, f) = hid_copies(tau, h)

        @pl.when(tau == zl)
        def _():
            own.start()
            f.start()

        @pl.when(tau != zl)
        def _():
            a.start()
            b.start()

    def partner_halo(h):
        for up in range(2):
            y_copy(oz, h, up).wait_recv()

        @pl.when(zl != c)
        def _():
            for dh in (0, 2):
                x_copy(h, dh).start()

        for dh in (0, 2):
            sib_copy(oz, h, dh).start()

    def inner(h):
        for tau in range(2):
            for dh in range(3):
                sib_copy(tau, h, dh).wait_recv()
        attend(1 - c, h)
        send_hidden(1 - c, h)

    def edge(h):
        for dh in range(3):
            x_copy(h, dh).wait_recv()
        attend(c, h)
        send_hidden(c, h)

    def wo_ready(q):
        for zz in range(2):
            wo_pair(wz.at[q, zz], me2, q, zz).wait_recv()

            @pl.when(holder)
            def _(zz=zz):
                wo_own(q, zz).wait()

    wo_ready(0)

    def wo_y(slot, i):
        ref = wo.at[slot, :, c, y]
        return o_copy(ref, ref, (yf, yb)[i], 14 + 2 * slot + i)

    wy = [wo_y(slot, i) for slot in range(2) for i in range(2)]
    for cp in wy:
        cp.start()
    o_sib = [[same(wo.at[slot, :, c, y], sib)] for slot in range(2)]
    partner_halo(0)
    inner(0)
    partner_halo(1)
    inner(1)
    partner_halo(2)
    edge(0)
    edge(1)
    inner(2)
    edge(2)

    for cp in started:
        cp.wait_send()
    drained = len(started)

    for q in range(2):
        for zz in range(2):
            wo_pair(wz.at[q, zz], me2, q, zz).wait_send()

            @pl.when(holder)
            def _(q=q, zz=zz):
                wo_next(q, zz).wait_send()

        @pl.when(holder)
        def _(q=q):
            wo_z(q, 0).wait_send()

        @pl.when(jnp.logical_not(holder))
        def _(q=q):
            wo_z(q, 1).wait_send()
            wo_z(q, 2).wait_send()

    def drain(h, carry):
        for tau in range(2):
            for up in range(2):
                y_copy(tau, h, up).wait_send()
            for dh in range(3):
                sib_copy(tau, h, dh).wait_send()
        for dh in range(3):
            x_copy(h, dh).wait_send()
        return carry

    lax.fori_loop(0, 3, drain, 0)

    wo_ready(1)
    for slot in range(2):
        o_sib[slot].append(same(wo.at[slot, :, c, wrap(y + 2)], sib))

    def hidden(h):
        own, remote = hid_copies(zl, h)
        own.wait()
        arrived(*remote)

    def mix(a, lo, n):
        lhs = jnp.concatenate([hid[:, i * 384 + lo : i * 384 + lo + n] for i in range(4)], 1)
        rhs = wo[a].reshape(768, 1536)
        rhs = jnp.concatenate([rhs[:, i * 384 + lo : i * 384 + lo + n] for i in range(4)], 1)
        return lax.dot_general(lhs, rhs, (((1,), (1,)), ((), ())), preferred_element_type=F32)

    for a in range(2):
        for i in range(2):
            arrived(wy[2 * a + i])
            o_sib[a].append(same(wo.at[a, :, c, wrap(y - df + 2 * df * i)], sib))
        arrived(*o_sib[a])
        if a == 0:
            hidden(0)
            hidden(1)
        acc[a] = mix(a, 0, 256)
    hidden(2)
    for a in range(2):
        r = (acc[a] + mix(a, 256, 128)).astype(BF)
        for f in range(2):
            for i in range(2):
                at = (2 * f + i) * 48
                out[0, f, i, :, a * 768 : a * 768 + 768] = r[at : at + 48]
                out[1, f, i, :, a * 768 : a * 768 + 768] = r[T + at : T + at + 48]

    for cp in started[drained:] + wy:
        cp.wait_send()
    for h in range(3):
        for cp in hid_copies(zl, h)[1]:
            cp.wait_send()


def per_device(tokens, tangent, qkv_weight, out_weight, reach):
    any_spec = pl.BlockSpec(memory_space=pl.ANY)
    vmem = pl.BlockSpec(memory_space=pltpu.VMEM)
    dma = pltpu.SemaphoreType.DMA
    both = pl.pallas_call(
        kernel,
        out_shape=pltpu.VMEM((2, 2, 2, 48, 1536), BF),
        in_specs=[pl.BlockSpec(memory_space=pltpu.SMEM)] + [any_spec] * 4,
        out_specs=vmem,
        scratch_shapes=[
            pltpu.VMEM((2, 2, T, D), BF),
            pltpu.VMEM((3, 2, 4, 2, 2, T, 128), BF),
            pltpu.VMEM((4, 2, 2, T, 384), BF),
            pltpu.VMEM((15, T, 1536), BF),
            pltpu.VMEM((2, 3, 2 * T, 256), BF),
            pltpu.VMEM((2, 2 * T, 384), BF),
            pltpu.VMEM((2 * T, 1536), BF),
            pltpu.VMEM((2, 2, QT, 1536), BF),
            pltpu.VMEM((2, 2, 2, 4, QT, 1536), BF),
            pltpu.VMEM((2, 2 * T, 768), F32),
            dma((15,)),
            dma((SENDS,)),
            dma((SENDS,)),
            dma((2, 18)),
            dma((2, 2, 3, 2)),
            dma((2, 3, 3)),
            dma((2, 2, 3, 3)),
            dma((2, 3, 3)),
        ],
        compiler_params=pltpu.CompilerParams(
            collective_id=0, has_side_effects=True, vmem_limit_bytes=60 * 1024 * 1024
        ),
    )(reach, tokens.reshape(T, D), tangent.reshape(T, D), jnp.transpose(qkv_weight, (1, 0, 2)), out_weight.T)
    return both[0], both[1]


def solution(mesh):
    in_specs = (
        P("tm", "height", None, None),
        P("tm", "height", None, None),
        P("tm", None, "mp"),
        P("mp", "tm"),
        P(None, "mp"),
    )
    out_specs = (P("tm", "height", None, "mp"), P("tm", "height", None, "mp"))
    return jax.shard_map(per_device, mesh=mesh, in_specs=in_specs, out_specs=out_specs, check_vma=False)
```
